128 devices in a mesh: row: 8 (over y_hi, z), col: 16 (over x, y_lo, core).
Axes of the slice: x: 4, y: 4 (y_hi: 2, y_lo: 2; y = y_hi * 2 + y_lo), z: 4, core: 2. Of those that a mesh axis runs over, the one named last changes fastest.
Arguments:
- homolog_features: bfloat16 [64, 704, 256], P('col', 'row'), may hold values from -6 to 6
- pair_state: bfloat16 [704, 704, 128], P('row', 'col'), may hold values from -6 to 6
- first_factor_matrix: bfloat16 [256, 32], replicated, may hold values from -0.375 to 0.375
- second_factor_matrix: bfloat16 [256, 32], replicated, may hold values from -0.375 to 0.375
- outer_pair_weight: bfloat16 [1024, 128], replicated, may hold values from -1.5 to 1.5
- triangle_left_weight: bfloat16 [128, 256], replicated, may hold values from -0.5 to 0.5
- triangle_right_weight: bfloat16 [128, 256], replicated, may hold values from -0.5 to 0.5
- triangle_gate_weight: bfloat16 [128, 128], replicated, may hold values from -0.5 to 0.5
- triangle_output_weight: bfloat16 [128, 128], replicated, may hold values from -0.5 to 0.5
Outputs:
- pair_out: bfloat16 [704, 704, 128], P('row', 'col')
The draws below stay inside these ranges and needn't reach their ends.
All inputs are finite; a program needn't handle non-finite values.
Results may differ from the reference program's by a relative error of at most 0.0069.
Values may be sent and summed in bfloat16 or wider, within the bound.
A program may use at most 128 MiB of HBM per device.

```python
import math
import jax
import jax.numpy as jnp
from jax import lax

FEATURE_DEPTH = 256
HIDDEN_FEATURES = 32
CZ = 128
CH = 128
HOMOLOG_TOTAL = 64
CHAIN_LENGTH = 704


def steps_of(key, extent, shards, smallest, largest):
    factor_of, own = 1.0, jax.random.fold_in(key, 6)
    for dim, parts in shards:
        steps = jnp.exp(jax.random.uniform(jax.random.fold_in(own, dim), (parts,), jnp.float32, smallest / len(shards), largest / len(shards)))
        factor_of = factor_of * jnp.repeat(steps, extent[dim] // parts).reshape([-1 if axis == dim else 1 for axis in range(len(extent))])
    return factor_of


def normal_values(own_key, dims, scale, most, split=(), kind=jnp.bfloat16):
    result = scale * jax.random.normal(own_key, dims, jnp.float32)
    if split:
        result = result * steps_of(own_key, dims, split, -0.22, 0.18)
    return jnp.clip(result, -most, most).astype(kind)


def setup_inputs(seed: int = 0) -> dict:
    key_of = jax.random.split(jax.random.key(seed), 10)
    return {
        "homolog_features": normal_values(key_of[0], (HOMOLOG_TOTAL, CHAIN_LENGTH, FEATURE_DEPTH), 1.0, 6.0, ((0, 16), (1, 8))),
        "pair_state": normal_values(key_of[1], (CHAIN_LENGTH, CHAIN_LENGTH, CZ), 1.0, 6.0, ((0, 8), (1, 16))),
        "first_factor_matrix": normal_values(key_of[2], (FEATURE_DEPTH, HIDDEN_FEATURES), FEATURE_DEPTH ** -0.5, 0.375),
        "second_factor_matrix": normal_values(key_of[3], (FEATURE_DEPTH, HIDDEN_FEATURES), FEATURE_DEPTH ** -0.5, 0.375),
        "outer_pair_weight": normal_values(key_of[4], (HIDDEN_FEATURES * HIDDEN_FEATURES, CZ), (HIDDEN_FEATURES * HIDDEN_FEATURES // HOMOLOG_TOTAL) ** -0.5, 1.5),
        "triangle_left_weight": normal_values(key_of[5], (CZ, 2 * CH), CZ ** -0.5, 0.5),
        "triangle_right_weight": normal_values(key_of[6], (CZ, 2 * CH), CZ ** -0.5, 0.5),
        "triangle_gate_weight": normal_values(key_of[7], (CZ, CZ), CZ ** -0.5, 0.5),
        "triangle_output_weight": normal_values(key_of[8], (CH, CZ), CH ** -0.5, 0.5),
    }


def apply_layer_norm(values, reduce_axis):
    average = lax.optimization_barrier(jnp.mean(values, axis=reduce_axis, keepdims=True))
    centered = values - average
    variance = lax.optimization_barrier(jnp.mean(centered * centered, axis=reduce_axis, keepdims=True))
    return centered * lax.rsqrt(variance + 1e-05)

def rounded_value(values):
    return lax.optimization_barrier(values.astype(jnp.bfloat16))

def reference(homolog_features, pair_state, first_factor_matrix, second_factor_matrix, outer_pair_weight, triangle_left_weight, triangle_right_weight, triangle_gate_weight, triangle_output_weight):
    alignment_norm = rounded_value(apply_layer_norm(homolog_features.astype(jnp.float32), -1)).astype(jnp.float32)
    left_alignment = rounded_value(jnp.einsum('mgu,ur->mgr', alignment_norm, first_factor_matrix.astype(jnp.float32))).astype(jnp.float32)
    right_alignment = rounded_value(jnp.einsum('mgu,ur->mgr', alignment_norm, second_factor_matrix.astype(jnp.float32))).astype(jnp.float32)
    block_slice = math.gcd(CHAIN_LENGTH, 64)
    weight_outer = outer_pair_weight.astype(jnp.float32)

    def outer_block(slice_index):
        left_block_slice = lax.dynamic_slice_in_dim(left_alignment, slice_index * block_slice, block_slice, 1)
        outer_sum = jnp.einsum('rhp,rmw->hmpw', left_block_slice, right_alignment) * (1.0 / HOMOLOG_TOTAL)
        flat = rounded_value(outer_sum).astype(jnp.float32).reshape(block_slice, CHAIN_LENGTH, HIDDEN_FEATURES * HIDDEN_FEATURES)
        return jnp.einsum('ijf,fz->ijz', flat, weight_outer)
    update = lax.map(outer_block, jnp.arange(CHAIN_LENGTH // block_slice, dtype=jnp.int32)).reshape(CHAIN_LENGTH, CHAIN_LENGTH, CZ)
    pair_mid = pair_state.astype(jnp.float32) + update
    pair_norm = rounded_value(apply_layer_norm(pair_mid, -1)).astype(jnp.float32)
    left_proj = jnp.einsum('ijd,dc->ijc', pair_norm, triangle_left_weight.astype(jnp.float32))
    right_proj = jnp.einsum('ijd,dc->ijc', pair_norm, triangle_right_weight.astype(jnp.float32))
    left_edge = rounded_value(jax.nn.sigmoid(left_proj[..., :CH]) * left_proj[..., CH:]).astype(jnp.float32)
    right_edge = rounded_value(jax.nn.sigmoid(right_proj[..., :CH]) * right_proj[..., CH:]).astype(jnp.float32)
    combined = jnp.einsum('ikc,jkc->ijc', left_edge, right_edge)
    combined_norm = rounded_value(apply_layer_norm(combined, -1)).astype(jnp.float32)
    gating = jax.nn.sigmoid(jnp.einsum('ijd,dz->ijz', pair_norm, triangle_gate_weight.astype(jnp.float32)))
    branch = jnp.einsum('ijc,cz->ijz', combined_norm, triangle_output_weight.astype(jnp.float32))
    return (pair_mid + gating * branch).astype(jnp.bfloat16)
```

```python
import jax
import jax.numpy as jnp
from jax import lax
from jax.experimental import pallas as pl
from jax.experimental.pallas import tpu as pltpu
from jax.sharding import PartitionSpec as P

ROWS, COLS = 8, 16
N = ROWS * COLS
RI, CJ = 88, 44
MESH = pl.DeviceIdType.MESH
VM = pl.BlockSpec(memory_space=pltpu.VMEM)
F32, BF = jnp.float32, jnp.bfloat16
NT = (((1,), (1,)), ((), ()))
TN = (((0,), (0,)), ((), ()))


def dev(flat):
    return (flat // COLS, flat % COLS)


def mixed(me, step):
    u = (step * 37) % 128
    a, b, c, dk = u % 4, (u // 4) % 4, (u // 16) % 4, u // 64
    row, col = me // COLS, me % COLS
    x, y, z, k = col // 4, (row // 4) * 2 + (col // 2) % 2, row % 4, col % 2
    x, y, z, k = (x + a) % 4, (y + a + b) % 4, (z + a + c) % 4, (k + dk) % 2
    return ((y // 2) * 4 + z) * COLS + x * 4 + (y % 2) * 2 + k


def sigmoid(v):
    return 0.5 * jnp.tanh(0.5 * v) + 0.5


def msa_kernel(hf, f1p, f2p, l_out, r_out, a_ref, p_ref, ls, rs, ssl, ssr, rsl, rsr):
    row, col = lax.axis_index("row"), lax.axis_index("col")
    sem = pltpu.get_barrier_semaphore()

    def greet(s, _):
        t = (col + s) % COLS
        pl.semaphore_signal(sem, inc=1, device_id=(row, t), device_id_type=MESH)
        return 0

    lax.fori_loop(1, COLS, greet, 0)

    def greet_source(s, _):
        own = jnp.logical_and(row == col // 2, s == col)

        @pl.when(jnp.logical_not(own))
        def _():
            pl.semaphore_signal(sem, inc=1, device_id=(col // 2, s), device_id_type=MESH)

        return 0

    lax.fori_loop(0, COLS, greet_source, 0)

    v = hf[...].astype(F32)
    centered = v - jnp.mean(v, axis=-1, keepdims=True)
    mn = centered * lax.rsqrt(jnp.mean(centered * centered, axis=-1, keepdims=True) + 1e-05)
    for s in range(4):
        for g in range(22):
            qt, q = g // 4, g % 4
            a_ref[qt * 16 + s * 4 : qt * 16 + s * 4 + 4, q * 256 : q * 256 + 256] = mn[s, g * 4 : g * 4 + 4]
    a_ref[80:96, 512:1024] = jnp.zeros((16, 512), F32)
    lm = jnp.dot(a_ref[...].astype(BF), f1p[...], preferred_element_type=F32)
    for qt in range(6):
        ls[:, qt * 128 : qt * 128 + 128] = lm[qt * 16 : qt * 16 + 16].astype(BF)
    pr = jnp.dot(
        jnp.concatenate([mn[s] for s in range(4)], axis=1).astype(BF), f2p[...], preferred_element_type=F32
    )
    p_ref[...] = jnp.zeros(p_ref.shape, F32)
    p_ref[0:44] = pr[0:44]
    p_ref[64:108] = pr[44:88]
    tr = p_ref[...].T
    for h in range(2):
        rs[h] = jnp.concatenate(
            [tr[eg * 16 : eg * 16 + 16, h * 64 : h * 64 + 48] for eg in range(8)], axis=1
        ).astype(BF)

    own_source = (row == col // 2).astype(jnp.int32)
    pl.semaphore_wait(sem, (COLS - 1) + 2 * ROWS - own_source)

    own = pl.ds(pl.multiple_of(col * 16, 16), 16)
    keep = pltpu.make_async_copy(ls, l_out.at[own], rsl)
    keep.start()

    def left(s):
        return pltpu.make_async_remote_copy(
            src_ref=ls, dst_ref=l_out.at[own], send_sem=ssl.at[s], recv_sem=rsl,
            device_id=(row, (col + s) % COLS), device_id_type=MESH,
        )

    def right(s):
        h, t = s % 2, (row + s // 2) % ROWS
        return pltpu.make_async_remote_copy(
            src_ref=rs.at[h], dst_ref=r_out.at[own], send_sem=ssr.at[s], recv_sem=rsr,
            device_id=(t, 2 * row + h), device_id_type=MESH,
        )

    def mine(s):
        return jnp.logical_and(s // 2 == 0, col == 2 * row + s % 2)

    def send_right(s, _):
        @pl.when(jnp.logical_not(mine(s)))
        def _():
            right(s).start()

        @pl.when(mine(s))
        def _():
            pltpu.make_async_copy(rs.at[s % 2], r_out.at[own], rsr).start()

        return 0

    def send_left(s, _):
        left(s).start()
        return 0

    lax.fori_loop(1, COLS, send_left, 0)
    lax.fori_loop(0, 2 * ROWS, send_right, 0)

    def sent_left(s, _):
        left(s).wait_send()
        return 0

    def sent_right(s, _):
        @pl.when(jnp.logical_not(mine(s)))
        def _():
            right(s).wait_send()

        return 0

    pltpu.make_async_copy(l_out, l_out, rsl).wait()
    pltpu.make_async_copy(r_out, r_out, rsr).wait()
    lax.fori_loop(1, COLS, sent_left, 0)
    lax.fori_loop(0, 2 * ROWS, sent_right, 0)


def iota(shape, dim):
    return lax.broadcasted_iota(jnp.int32, shape, dim)


def pair_kernel(lmsg, rmsg, ps, wt, wedge, wgate, send, mid, gate, rmt, bd, lhs, osc, pn, el, er):
    rmt[...] = rmsg[...].T
    bd[...] = jnp.zeros(bd.shape, BF)

    def place(e, _):
        for q in range(4):
            bd[pl.ds(pl.multiple_of(e * 128 + q * 32, 32), 32), q * 128 : q * 128 + 128] = wt[
                pl.ds(pl.multiple_of(e * 32, 32), 32), :
            ]
        return 0

    lax.fori_loop(0, 32, place, 0)

    def outer(uw, _):
        u, w = uw // 4, uw % 4
        a, b = iota((256, 256), 0), iota((256, 256), 1)
        pick = (a // 4 == b // 4) & (a % 4 == w) & (b % 4 == u)
        sel = jnp.dot(rmt[...], pick.astype(F32).astype(BF), preferred_element_type=F32).astype(BF)
        x = jnp.dot(sel, lmsg[...], preferred_element_type=F32) * (1.0 / 64)
        for eg in range(8):
            for qt in range(6):
                lhs[
                    pl.ds(pl.multiple_of(u * 288 + qt * 48, 16), 48),
                    pl.ds(pl.multiple_of(w * 1024 + eg * 128, 128), 128),
                ] = x[eg * 48 : eg * 48 + 48, qt * 128 : qt * 128 + 128].astype(BF)
        return 0

    lax.fori_loop(0, 16, outer, 0)

    def project(u, _):
        rows = pl.ds(pl.multiple_of(u * 288, 16), 288)
        osc[rows, :] = jnp.dot(lhs[rows, :], bd[...], preferred_element_type=F32)
        return 0

    lax.fori_loop(0, 4, project, 0)

    def normalize(ia, _):
        for ib in range(11):
            upd = osc[
                pl.ds(pl.multiple_of((ia % 4) * 288 + (ib // 2) * 48, 8), 48),
                pl.ds(pl.multiple_of((ib % 2) * 256 + (ia // 4) * 128, 128), 128),
            ][:44]
            m = ps[8 * ib + ia].astype(F32) + upd
            mid[8 * ib + ia] = m
            c = m - jnp.mean(m, axis=-1, keepdims=True)
            n = c * lax.rsqrt(jnp.mean(c * c, axis=-1, keepdims=True) + 1e-05)
            pn[ia, 44 * ib : 44 * ib + 44] = n
        pn[ia, 484:512] = jnp.zeros((28, 128), F32)
        p = pn[ia].astype(BF)
        proj = lax.dot_general(wedge[...], p, NT, preferred_element_type=F32)
        left = sigmoid(proj[0:128]) * proj[128:256]
        right = sigmoid(proj[256:384]) * proj[384:512]
        rows = pl.ds(pl.multiple_of(ia * 128, 128), 128)
        for t in range(4):
            el[t, rows, :] = left[:, t * 128 : t * 128 + 128]
            er[t, rows, :] = right[:, t * 128 : t * 128 + 128]
        gate[ia] = sigmoid(jnp.dot(p, wgate[...], preferred_element_type=F32))
        return 0

    lax.fori_loop(0, 8, normalize, 0)

    def pack(c, _):
        for side, e in ((0, el), (32, er)):
            send[c, side : side + 32] = jnp.concatenate(
                [e[t, pl.ds(c, 8, stride=128), :] for t in range(4)], axis=0
            ).astype(BF)
        return 0

    lax.fori_loop(0, 128, pack, 0)


def triangle_kernel(send, out, rbuf, sb, s_ref, perm, lh, rh, lop, rop, lhs2, ob, ss, rsem, ls, ss2, rsem2):
    me = lax.axis_index("row") * COLS + lax.axis_index("col")
    sem = pltpu.get_barrier_semaphore()

    def greet(s, _):
        pl.semaphore_signal(sem, inc=1, device_id=dev((me + s) % N), device_id_type=MESH)
        return 0

    lax.fori_loop(1, N, greet, 0)
    pl.semaphore_wait(sem, N - 1)
    keep = pltpu.make_async_copy(send.at[me], rbuf.at[me], ls)
    keep.start()

    def scatter(s, _):
        t = mixed(me, s)
        pltpu.make_async_remote_copy(
            src_ref=send.at[t], dst_ref=rbuf.at[me], send_sem=ss, recv_sem=rsem, device_id=dev(t), device_id_type=MESH
        ).start()
        return 0

    lax.fori_loop(1, N, scatter, 0)

    def spread(b, _):
        f, n = iota((1024, 128), 0), iota((1024, 128), 1)
        k = n % 64
        hit = (f // 512 == n // 64) & (f % 512 == 44 * b + k) & (k < 44)
        s_ref[:, pl.ds(pl.multiple_of(b * 128, 128), 128)] = hit.astype(F32).astype(BF)
        return 0

    lax.fori_loop(0, 11, spread, 0)

    def columns(t, _):
        m, n = iota((704, 128), 0), iota((704, 128), 1) + t * 128
        j = 88 * ((m // 8) % 8) + 8 * (m // 64) + m % 8
        hit = (j == 44 * (n // 64) + n % 64) & (n % 64 < 44)
        perm[:, pl.ds(pl.multiple_of(t * 128, 128), 128)] = hit.astype(F32).astype(BF)
        return 0

    lax.fori_loop(0, 8, columns, 0)
    keep.wait()
    whole = pltpu.make_async_remote_copy(
        src_ref=send.at[pl.ds(0, N - 1)], dst_ref=rbuf.at[pl.ds(0, N - 1)], send_sem=ss, recv_sem=rsem,
        device_id=dev((me + 1) % N), device_id_type=MESH,
    )
    whole.wait_recv()

    def unpack(s, _):
        r, cc = s // COLS, s % COLS
        msg = rbuf[s].astype(F32)
        rows = pl.ds(pl.multiple_of((cc // 2) * 64 + r * 8, 8), 8)
        for t in range(4):
            lanes = pl.ds(pl.multiple_of((cc % 2) * 512 + t * 128, 128), 128)
            lh[rows, lanes] = msg[t * 8 : t * 8 + 8]
            rh[rows, lanes] = msg[32 + t * 8 : 40 + t * 8]
        return 0

    lax.fori_loop(0, N, unpack, 0)

    for src, dst in ((lh, lop), (rh, rop)):
        m = src[...].astype(BF)

        def widen(b, _, m=m, dst=dst):
            x = jnp.dot(m, s_ref[:, pl.ds(pl.multiple_of(b * 128, 128), 128)], preferred_element_type=F32).astype(BF)
            for p in range(8):
                dst[pl.ds(pl.multiple_of(b * 64, 64), 64), p * 128 : p * 128 + 128] = x[p * 64 : p * 64 + 64]
            return 0

        lax.fori_loop(0, 11, widen, 0)

    def product(b, _):
        rows = pl.ds(pl.multiple_of(b * 64, 64), 64)
        c = lax.dot_general(lop[rows, :], rop[...], NT, preferred_element_type=F32).astype(BF)
        d = jnp.dot(c, perm[...], preferred_element_type=F32).astype(BF)
        for p in range(8):
            lhs2[p * 64 : p * 64 + 64, pl.ds(pl.multiple_of(b * 128, 128), 128)] = d[:, p * 128 : p * 128 + 128]
        return 0

    lax.fori_loop(0, 11, product, 0)
    ob[...] = lax.dot_general(lhs2[...], s_ref[...], NT, preferred_element_type=F32)

    def repack(s, _):
        r, cc = s // COLS, s % COLS
        rows = pl.ds(pl.multiple_of((cc // 2) * 64 + r * 8, 8), 8)
        sb[s] = jnp.concatenate(
            [ob[rows, pl.ds(pl.multiple_of((cc % 2) * 512 + t * 128, 128), 128)] for t in range(4)], axis=0
        ).astype(BF)
        return 0

    lax.fori_loop(0, N, repack, 0)
    back = pltpu.make_async_copy(sb.at[me], out.at[me], ls)
    back.start()

    def scatter_back(s, _):
        t = mixed(me, s)
        pltpu.make_async_remote_copy(
            src_ref=sb.at[t], dst_ref=out.at[me], send_sem=ss2, recv_sem=rsem2, device_id=dev(t), device_id_type=MESH
        ).start()
        return 0

    lax.fori_loop(1, N, scatter_back, 0)
    back.wait()
    whole.wait_send()
    whole2 = pltpu.make_async_remote_copy(
        src_ref=sb.at[pl.ds(0, N - 1)], dst_ref=out.at[pl.ds(0, N - 1)], send_sem=ss2, recv_sem=rsem2,
        device_id=dev((me + 1) % N), device_id_type=MESH,
    )
    whole2.wait_recv()
    whole2.wait_send()


def finish_kernel(recv, mid, gate, wo, out, rc, br):
    def unpack(c, _):
        x = recv[c].astype(F32)
        for t in range(4):
            rc[t, pl.ds(pl.multiple_of(c * 8, 8), 8), :] = x[t * 8 : t * 8 + 8]
        return 0

    lax.fori_loop(0, N, unpack, 0)

    def finish(ia, _):
        for t in range(4):
            z = rc[t, pl.ds(ia, 128, stride=8), :]
            c = z - jnp.mean(z, axis=0, keepdims=True)
            n = (c * lax.rsqrt(jnp.mean(c * c, axis=0, keepdims=True) + 1e-05)).astype(BF)
            branch = lax.dot_general(n, wo[...], TN, preferred_element_type=F32)
            br[t * 128 : t * 128 + 128] = branch * gate[ia, t * 128 : t * 128 + 128]
        for ib in range(11):
            out[8 * ib + ia] = (mid[8 * ib + ia] + br[44 * ib : 44 * ib + 44]).astype(BF)
        return 0

    lax.fori_loop(0, 8, finish, 0)


def params(**kw):
    return pltpu.CompilerParams(vmem_limit_bytes=56 * 2**20, **kw)


def per_device(hf, ps, f1, f2, wo, wl, wr, wg, wout):
    eye = jnp.eye(4, dtype=BF)
    f1p = (eye[:, None, :, None] * f1[None, :, None, :]).reshape(1024, 128)
    f2r = f2.reshape(256, 4, 8).transpose(0, 2, 1)
    f2p = (eye[:, None, None, :, None] * f2r[None, :, :, None, :]).reshape(1024, 128)
    wt = wo.reshape(32, 32, 128).transpose(1, 0, 2).reshape(1024, 128)
    wedge = jnp.concatenate([wl, wr], axis=1).T
    dma = pltpu.SemaphoreType.DMA
    sds = jax.ShapeDtypeStruct
    lmsg, rmsg = pl.pallas_call(
        msa_kernel,
        out_shape=(sds((256, 768), BF), sds((256, 384), BF)),
        in_specs=[VM] * 3,
        out_specs=(VM, VM),
        scratch_shapes=[
            pltpu.VMEM((96, 1024), F32), pltpu.VMEM((128, 128), F32), pltpu.VMEM((16, 768), BF),
            pltpu.VMEM((2, 16, 384), BF), dma((16,)), dma((16,)), dma, dma,
        ],
        compiler_params=params(collective_id=0, has_side_effects=True),
    )(hf, f1p, f2p)
    send, mid, gate = pl.pallas_call(
        pair_kernel,
        out_shape=(sds((N, 64, 128), BF), sds((RI, CJ, 128), F32), sds((8, 512, 128), F32)),
        in_specs=[VM] * 6,
        out_specs=(VM, VM, VM),
        scratch_shapes=[
            pltpu.VMEM((384, 256), BF), pltpu.VMEM((4096, 512), BF), pltpu.VMEM((1152, 4096), BF),
            pltpu.VMEM((1152, 512), F32), pltpu.VMEM((8, 512, 128), F32), pltpu.VMEM((4, 1024, 128), F32),
            pltpu.VMEM((4, 1024, 128), F32),
        ],
        compiler_params=params(),
    )(lmsg, rmsg, ps, wt, wedge, wg)
    recv = pl.pallas_call(
        triangle_kernel,
        out_shape=sds((N, 32, 128), BF),
        in_specs=[VM],
        out_specs=VM,
        scratch_shapes=[
            pltpu.VMEM((N, 64, 128), BF), pltpu.VMEM((N, 32, 128), BF), pltpu.VMEM((1024, 1408), BF),
            pltpu.VMEM((704, 1024), BF), pltpu.VMEM((512, 1024), F32), pltpu.VMEM((512, 1024), F32),
            pltpu.VMEM((704, 1024), BF), pltpu.VMEM((704, 1024), BF), pltpu.VMEM((512, 1408), BF),
            pltpu.VMEM((512, 1024), F32), dma, dma, dma, dma, dma,
        ],
        compiler_params=params(collective_id=1, has_side_effects=True),
    )(send)
    return pl.pallas_call(
        finish_kernel,
        out_shape=sds((RI, CJ, 128), BF),
        in_specs=[VM] * 4,
        out_specs=VM,
        scratch_shapes=[pltpu.VMEM((4, 1024, 128), F32), pltpu.VMEM((512, 128), F32)],
        compiler_params=params(),
    )(recv, mid, gate, wout)


def solution(mesh):
    return jax.shard_map(
        per_device,
        mesh=mesh,
        in_specs=(P("col", "row", None), P("row", "col", None), P(), P(), P(), P(), P(), P(), P()),
        out_specs=P("row", "col", None),
        check_vma=False,
    )
```

```python
import jax
import jax.numpy as jnp
from jax import lax
from jax.experimental import pallas as pl
from jax.experimental.pallas import tpu as pltpu
from jax.sharding import PartitionSpec as P

ROWS, COLS = 8, 16
N = ROWS * COLS
RI, CJ = 88, 44
PITCH, PITCH2 = 136, 24
MESH = pl.DeviceIdType.MESH
VM = pl.BlockSpec(memory_space=pltpu.VMEM)
F32, BF = jnp.float32, jnp.bfloat16
NT = (((1,), (1,)), ((), ()))
TN = (((0,), (0,)), ((), ()))
SPAN = ((0, 3), (2, 6), (5, 9), (8, 11))


def dev(flat):
    return (flat // COLS, flat % COLS)


def shifted(me, a, b, c, dk):
    row, col = me // COLS, me % COLS
    x, y, z, k = col // 4, (row // 4) * 2 + (col // 2) % 2, row % 4, col % 2
    x, y, z, k = (x + a) % 4, (y + b) % 4, (z + c) % 4, (k + dk) % 2
    return ((y // 2) * 4 + z) * COLS + x * 4 + (y % 2) * 2 + k


def mixed(me, step):
    u = (step * 37) % 128
    a, b, c, dk = u % 4, (u // 4) % 4, (u // 16) % 4, u // 64
    return shifted(me, a, a + b, a + c, dk)


def sigmoid(v):
    return 0.5 * jnp.tanh(0.5 * v) + 0.5


def iota(shape, dim):
    return lax.broadcasted_iota(jnp.int32, shape, dim)


def ones_where(mask):
    return mask.astype(F32).astype(BF)


def at(start, size, align):
    return pl.ds(pl.multiple_of(start, align), size)


def kernel(
    hf, ps, f1, f2, wo, wl, wr, wg, wout, out,
    a_ref, p_ref, ls, rs32, rs, lmsg, rt, rmsg, rmt, wof, bd, lhs, osc, psf, pn, el, er, wedge, gate,
    send, lh, sw, s2, lop, rop32, rop, lhs2, sb, rv, rc, br,
    l_send, l_recv, r1_send, r1_recv, r2_send, r2_recv, e_send, e_recv, c_send, c_recv,
):
    row, col = lax.axis_index("row"), lax.axis_index("col")
    me = row * COLS + col
    sem = pltpu.get_barrier_semaphore()

    def greet(s, _):
        pl.semaphore_signal(sem, inc=1, device_id=dev((me + s) % N), device_id_type=MESH)
        return 0

    lax.fori_loop(1, N, greet, 0)

    v = hf[...].astype(F32)
    centered = v - jnp.mean(v, axis=-1, keepdims=True)
    mn = centered * lax.rsqrt(jnp.mean(centered * centered, axis=-1, keepdims=True) + 1e-05)
    for s in range(4):
        for g in range(22):
            qt, q = g // 4, g % 4
            a_ref[qt * 16 + s * 4 : qt * 16 + s * 4 + 4, q * 256 : q * 256 + 256] = mn[s, g * 4 : g * 4 + 4]
    a_ref[80:96, 512:1024] = jnp.zeros((16, 512), F32)
    lm = jnp.concatenate(
        [
            jnp.dot(a_ref[:, q * 256 : q * 256 + 256].astype(BF), f1[...], preferred_element_type=F32)
            for q in range(4)
        ],
        axis=1,
    )
    for qt in range(6):
        ls[:, qt * 128 : qt * 128 + 128] = lm[qt * 16 : qt * 16 + 16].astype(BF)
    pr = jnp.concatenate(
        [jnp.dot(mn[s].astype(BF), f2[...], preferred_element_type=F32) for s in range(4)], axis=1
    )
    p_ref[...] = jnp.zeros(p_ref.shape, F32)
    p_ref[0:44] = pr[0:44]
    p_ref[64:108] = pr[44:88]
    tr = p_ref[...].T
    for h in range(2):
        for s in range(4):
            rs32[h, s * 4 : s * 4 + 4, :] = jnp.concatenate(
                [tr[s * 32 + eg * 4 : s * 32 + eg * 4 + 4, h * 64 : h * 64 + 48] for eg in range(8)], axis=1
            )
    rs[...] = rs32[...].astype(BF)
    pl.semaphore_wait(sem, N - 1)

    own = at(col * 16, 16, 16)
    pltpu.make_async_copy(ls, lmsg.at[own], l_recv).start()
    pltpu.make_async_copy(rs, rt.at[row], r1_recv).start()

    def send_right(s, _):
        pltpu.make_async_remote_copy(
            src_ref=rs, dst_ref=rt.at[row], send_sem=r1_send, recv_sem=r1_recv,
            device_id=((row + s) % ROWS, col), device_id_type=MESH,
        ).start()
        return 0

    lax.fori_loop(1, ROWS, send_right, 0)

    def send_left(s, _):
        pltpu.make_async_remote_copy(
            src_ref=ls, dst_ref=lmsg.at[own], send_sem=l_send, recv_sem=l_recv,
            device_id=(row, (col + s) % COLS), device_id_type=MESH,
        ).start()
        return 0

    lax.fori_loop(1, COLS, send_left, 0)

    wof[...] = wo[...].astype(F32)
    bd[...] = jnp.zeros(bd.shape, BF)

    def place(b, _):
        w = wof[pl.ds((b % 8) * 4 + b // 8, 32, stride=32), :].astype(BF)
        for q in range(4):
            bd[at(b * 128 + q * 32, 32, 32), q * 128 : q * 128 + 128] = w
        return 0

    lax.fori_loop(0, 32, place, 0, unroll=4)
    pltpu.make_async_copy(rt, rt, r1_recv).wait()
    own_half = pltpu.make_async_copy(rt.at[col // 2, col % 2], rmsg.at[own], r2_recv)
    own_half.start()

    def forward_right(s, _):
        t = (col + s) % COLS
        pltpu.make_async_remote_copy(
            src_ref=rt.at[t // 2, t % 2], dst_ref=rmsg.at[own], send_sem=r2_send, recv_sem=r2_recv,
            device_id=(row, t), device_id_type=MESH,
        ).start()
        return 0

    lax.fori_loop(1, COLS, forward_right, 0)
    psf[...] = ps[...].reshape(CJ * RI, 128).astype(F32)
    wedge[0:256] = wl[...].T
    wedge[256:512] = wr[...].T
    pltpu.make_async_copy(rmsg, rmsg, r2_recv).wait()
    pltpu.make_async_copy(lmsg, lmsg, l_recv).wait()

    rmt[...] = rmsg[...].T

    def outer(u, _):
        a, b = iota((256, 256), 0), iota((256, 256), 1)
        for w in range(4):
            pick = ones_where((a // 4 == b // 4) & (a % 4 == w) & (b % 4 == u))
            sel = jnp.dot(rmt[...], pick, preferred_element_type=F32).astype(BF)
            x = jnp.dot(sel, lmsg[...], preferred_element_type=F32) * (1.0 / 64)
            for eg in range(8):
                for qt in range(6):
                    lhs[at(u * 288 + qt * 48, 48, 16), w * 1024 + eg * 128 : w * 1024 + eg * 128 + 128] = x[
                        eg * 48 : eg * 48 + 48, qt * 128 : qt * 128 + 128
                    ].astype(BF)
        return 0

    lax.fori_loop(0, 4, outer, 0)

    def project(u, _):
        rows = at(u * 288, 288, 16)
        osc[rows, :] = jnp.dot(lhs[rows, :], bd[...], preferred_element_type=F32)
        return 0

    lax.fori_loop(0, 4, project, 0)

    for half in range(2):
        lo, hi = (0, 6) if half == 0 else (6, 11)

        def normalize(ia, _, lo=lo, hi=hi, half=half):
            for ib in range(lo, hi):
                i = 11 * ia + ib
                upd = osc[at((i % 4) * 288 + (i // 16) * 48, 48, 8), at((i % 16) // 4 * 128, 128, 128)][:44]
                cells = pl.ds(i, CJ, stride=RI)
                m = psf[cells, :] + upd
                psf[cells, :] = m
                c = m - jnp.mean(m, axis=-1, keepdims=True)
                n = c * lax.rsqrt(jnp.mean(c * c, axis=-1, keepdims=True) + 1e-05)
                pn[ia, 44 * ib : 44 * ib + 44] = n
            if half:
                pn[ia, 484:512] = jnp.zeros((28, 128), F32)
            p = pn[ia, half * 256 : half * 256 + 256].astype(BF)
            proj = lax.dot_general(wedge[...], p, NT, preferred_element_type=F32)
            left = sigmoid(proj[0:128]) * proj[128:256]
            right = sigmoid(proj[256:384]) * proj[384:512]
            rows = at(ia * PITCH, 128, 8)
            for t in range(2):
                el[t, rows, :] = left[:, t * 128 : t * 128 + 128]
                er[t, rows, :] = right[:, t * 128 : t * 128 + 128]
            return 0

        lax.fori_loop(0, 8, normalize, 0)

        def pack(c, _, half=half):
            for t in range(2):
                cells = pl.ds(c, 8, stride=PITCH)
                send[c, 2 * half + t] = jnp.concatenate([el[t, cells, :], er[t, cells, :]], axis=0).astype(BF)
            return 0

        lax.fori_loop(0, N, pack, 0, unroll=8)
        cells = lh.at[2 * half : 2 * half + 2, at(((col // 2) * 8 + row) * 16, 16, 16), at(col % 2 * 128, 128, 128)]
        pltpu.make_async_copy(send.at[me, 2 * half : 2 * half + 2], cells, e_recv.at[half]).start()

        def scatter(s, _, half=half, cells=cells):
            t = mixed(me, s)
            pltpu.make_async_remote_copy(
                src_ref=send.at[t, 2 * half : 2 * half + 2], dst_ref=cells, send_sem=e_send.at[half],
                recv_sem=e_recv.at[half], device_id=dev(t), device_id_type=MESH,
            ).start()
            return 0

        lax.fori_loop(1, N, scatter, 0)

    for t in range(4):
        lo, hi = SPAN[t]
        for b in range(lo, hi):
            f, n = iota((256, 128), 0), iota((256, 128), 1)
            k = n % 64
            hit = (f // 128 == n // 64) & (f % 128 + 128 * t == 44 * b + k) & (k < 44)
            sw[t, :, (b - lo) * 128 : (b - lo) * 128 + 128] = ones_where(hit)
            n, f = iota((128, 256), 0), iota((128, 256), 1)
            k = n % 16
            hit = (f // 128 == n // 64) & (f % 128 + 128 * t == 44 * b + 11 * (n % 64 // 16) + k) & (k < 11)
            s2[t, (b - lo) * 128 : (b - lo) * 128 + 128, :] = ones_where(hit)
    rop32[...] = jnp.zeros(rop32.shape, F32)

    def gates(ia, _):
        gate[ia] = sigmoid(jnp.dot(pn[ia].astype(BF), wg[...], preferred_element_type=F32))
        return 0

    lax.fori_loop(0, 8, gates, 0)

    for half in range(2):
        part = lh.at[2 * half : 2 * half + 2]
        pltpu.make_async_copy(part, part, e_recv.at[half]).wait()

    def widen(m, _):
        ys = []
        for t in range(4):
            lo, hi = SPAN[t]
            ys.append(
                jnp.dot(lh[t, at(m * 256, 256, 256), :], sw[t, :, : (hi - lo) * 128], preferred_element_type=F32)
            )
        for b in range(11):
            x = None
            for t in range(4):
                lo, hi = SPAN[t]
                if lo <= b < hi:
                    y = ys[t][:, (b - lo) * 128 : (b - lo) * 128 + 128]
                    x = y if x is None else x + y
            x = x.reshape(2, 8, 2, 8, 128)
            for q in range(2):
                p = 2 * m + q
                lop[b * 64 : b * 64 + 64, at(p * 128, 128, 128)] = x[q, :, 0].reshape(64, 128).astype(BF)
                for r in range(8):
                    rop32[p, pl.ds(r * 128 + b, 8, stride=16), :] = x[q, r, 1]
        return 0

    lax.fori_loop(0, 4, widen, 0)
    for p in range(8):
        rop[:, p * 128 : p * 128 + 128] = rop32[p].astype(BF)

    x0 = col // 4

    def product(step, _):
        dx = (step + 2) % 4
        g = (x0 + dx) % 4
        c = lax.dot_general(lop[...], rop[at(g * 256, 256, 256), :], NT, preferred_element_type=F32).astype(BF)
        for q in range(2):
            for b in range(11):
                lhs2[q * 64 : q * 64 + 64, b * 128 : b * 128 + 128] = c[b * 64 : b * 64 + 64, q * 128 : q * 128 + 128]
        zs = []
        for t in range(4):
            lo, hi = SPAN[t]
            z = jnp.dot(lhs2[:, lo * 128 : hi * 128], s2[t, : (hi - lo) * 128, :], preferred_element_type=F32)
            zs.append(z.reshape(16, 8, 256))
        for h in range(2):
            z = jnp.concatenate([zs[2 * h], zs[2 * h + 1]], axis=1).astype(BF)
            sb[h, at(g * 16, 16, 16)] = z

        def scatter_back(s, _):
            u = (s * 5 + step) % 32
            t = shifted(me, dx, u % 4, (u // 4 + u) % 4, u // 16)
            r, cc = t // COLS, t % COLS

            @pl.when(t != me)
            def _():
                pltpu.make_async_remote_copy(
                    src_ref=sb.at[:, cc // 2 * 8 + r, :, at(cc % 2 * 128, 128, 128)], dst_ref=rv.at[me],
                    send_sem=c_send, recv_sem=c_recv, device_id=dev(t), device_id_type=MESH,
                ).start()

            return 0

        lax.fori_loop(0, 32, scatter_back, 0)
        return 0

    lax.fori_loop(0, 4, product, 0)
    back = sb.at[:, col // 2 * 8 + row, :, at(col % 2 * 128, 128, 128)]
    pltpu.make_async_copy(back, rv.at[me], c_recv).start()
    pltpu.make_async_copy(rv, rv, c_recv).wait()

    def unpack(c, _):
        for h in range(2):
            rc[h, at(c * PITCH2, 16, 8), :] = rv[c, h].astype(F32)
        return 0

    lax.fori_loop(0, N, unpack, 0, unroll=8)

    def finish(ia, _):
        for t in range(4):
            z = rc[t // 2, pl.ds(t % 2 * 8 + ia, 128, stride=PITCH2), :]
            c = z - jnp.mean(z, axis=0, keepdims=True)
            n = (c * lax.rsqrt(jnp.mean(c * c, axis=0, keepdims=True) + 1e-05)).astype(BF)
            branch = lax.dot_general(n, wout[...], TN, preferred_element_type=F32)
            br[t * 128 : t * 128 + 128] = branch * gate[ia, t * 128 : t * 128 + 128]
        for ib in range(11):
            cells = pl.ds(11 * ia + ib, CJ, stride=RI)
            psf[cells, :] = psf[cells, :] + br[44 * ib : 44 * ib + 44]
        return 0

    lax.fori_loop(0, 8, finish, 0)
    out[...] = psf[...].astype(BF).reshape(CJ, RI, 128)

    def sent(src, sem):
        pltpu.make_async_remote_copy(
            src_ref=src, dst_ref=src, send_sem=sem, recv_sem=l_recv, device_id=dev((me + 1) % N), device_id_type=MESH
        ).wait_send()

    sent(lmsg.at[0:240], l_send)
    sent(rt.at[0:7], r1_send)
    sent(rmsg.at[0:240], r2_send)
    for half in range(2):
        sent(send.at[0 : N - 1, 0:2], e_send.at[half])
    sent(rv.at[0 : N - 1], c_send)


def per_device(hf, ps, f1, f2, wo, wl, wr, wg, wout):
    dma = pltpu.SemaphoreType.DMA
    vm = pltpu.VMEM
    out = pl.pallas_call(
        kernel,
        out_shape=jax.ShapeDtypeStruct((CJ, RI, 128), BF),
        in_specs=[VM] * 9,
        out_specs=VM,
        scratch_shapes=[
            vm((96, 1024), F32), vm((128, 128), F32), vm((16, 768), BF), vm((2, 16, 384), F32), vm((2, 16, 384), BF),
            vm((256, 768), BF), vm((8, 2, 16, 384), BF), vm((256, 384), BF), vm((384, 256), BF), vm((1024, 128), F32),
            vm((4096, 512), BF), vm((1152, 4096), BF), vm((1152, 512), F32), vm((CJ * RI, 128), F32),
            vm((8, 512, 128), F32), vm((2, 8 * PITCH, 128), F32), vm((2, 8 * PITCH, 128), F32), vm((512, 128), BF),
            vm((8, 512, 128), F32), vm((N, 4, 16, 128), BF), vm((4, 1024, 256), BF), vm((4, 256, 512), BF),
            vm((4, 512, 256), BF), vm((704, 1024), BF), vm((8, 1024, 128), F32), vm((1024, 1024), BF),
            vm((128, 1408), BF), vm((2, 64, 16, 256), BF), vm((N, 2, 16, 128), BF), vm((2, N * PITCH2, 128), F32),
            vm((512, 128), F32),
            dma, dma, dma, dma, dma, dma, dma((2,)), dma((2,)), dma, dma,
        ],
        compiler_params=pltpu.CompilerParams(
            vmem_limit_bytes=60 * 2**20, collective_id=0, has_side_effects=True
        ),
    )(hf, ps.transpose(1, 0, 2), f1, f2, wo, wl, wr, wg, wout)
    return out.transpose(1, 0, 2)


def solution(mesh):
    return jax.shard_map(
        per_device,
        mesh=mesh,
        in_specs=(P("col", "row", None), P("row", "col", None), P(), P(), P(), P(), P(), P(), P()),
        out_specs=P("row", "col", None),
        check_vma=False,
    )
```

```python
import jax
import jax.numpy as jnp
from jax import lax
from jax.experimental import pallas as pl
from jax.experimental.pallas import tpu as pltpu
from jax.sharding import PartitionSpec as P

ROWS, COLS = 8, 16
N = ROWS * COLS
RI, CJ = 88, 44
PITCH, PITCH2 = 136, 24
MESH = pl.DeviceIdType.MESH
VM = pl.BlockSpec(memory_space=pltpu.VMEM)
F32, BF = jnp.float32, jnp.bfloat16
NT = (((1,), (1,)), ((), ()))
TN = (((0,), (0,)), ((), ()))
SPAN = ((0, 3), (2, 6), (5, 9), (8, 11))


def in_half(a, b):
    return 6 * a + b if b < 6 else 24 + 5 * a + b - 6


def slot(ia, ib):
    i = in_half(ia % 4, ib)
    first = i // 4 if ib < 6 else i // 4 + 6
    return first + (ia // 4) * (6 if ib < 6 else 5), i % 4


def group_rows(g):
    return 4 * (g if g < 6 else g + 5 if g < 12 else g - 6 if g < 17 else g)


def dev(flat):
    return (flat // COLS, flat % COLS)


def sigmoid(v):
    return 0.5 * jnp.tanh(0.5 * v) + 0.5


def iota(shape, dim):
    return lax.broadcasted_iota(jnp.int32, shape, dim)


def ones_where(mask):
    return mask.astype(F32).astype(BF)


def at(start, size, align):
    return pl.ds(pl.multiple_of(start, align), size)


def kernel(
    hf, ps, f1, f2, wo, wl, wr, wg, wout, out,
    a_ref, p_ref, ls, rs32, rs, lmsg, rt, rmsg, rmt, wof, bd, lhs, osc, psf, pn, el, er, wedge, gate,
    send, lh, sw, s2, lop, rop32, rop, lhs2, sb, rv, rc, br,
    l_send, l_recv, r1_send, r1_recv, r2_send, r2_recv, e_send, e_recv, c_send, c_recv,
):
    row, col = lax.axis_index("row"), lax.axis_index("col")
    me = row * COLS + col
    around = [lax.rem(col + c, COLS) for c in range(COLS)]
    x, y = col // 4, row // 4 * 2 + col // 2 % 2
    x_col = [lax.rem(x + d, 4) * 4 for d in range(4)]
    y_col = [lax.rem(lax.rem(y + d, 4), 2) * 2 for d in range(4)]
    y_row = [lax.div(lax.rem(y + d, 4), 2) * 4 for d in range(4)]
    sem = pltpu.get_barrier_semaphore()

    def greet(o, _):
        r = lax.rem(row + o, ROWS)
        for c in range(COLS):
            if c:
                pl.semaphore_signal(sem, inc=1, device_id=(r, around[c]), device_id_type=MESH)
            else:

                @pl.when(o > 0)
                def _():
                    pl.semaphore_signal(sem, inc=1, device_id=(r, col), device_id_type=MESH)

        return 0

    lax.fori_loop(0, ROWS, greet, 0)

    v = hf[...].astype(F32)
    centered = v - jnp.mean(v, axis=-1, keepdims=True)
    mn = centered * lax.rsqrt(jnp.mean(centered * centered, axis=-1, keepdims=True) + 1e-05)
    for s in range(4):
        for g in range(22):
            qt, q = g // 4, g % 4
            a_ref[qt * 16 + s * 4 : qt * 16 + s * 4 + 4, q * 256 : q * 256 + 256] = mn[
                s, group_rows(g) : group_rows(g) + 4
            ]
    a_ref[80:96, 512:1024] = jnp.zeros((16, 512), F32)
    lm = jnp.concatenate(
        [
            lax.dot_general(a_ref[:, q * 256 : q * 256 + 256].astype(BF), f1[...], NT, preferred_element_type=F32)
            for q in range(4)
        ],
        axis=1,
    )
    for qt in range(6):
        ls[:, qt * 128 : qt * 128 + 128] = lm[qt * 16 : qt * 16 + 16].astype(BF)
    pr = jnp.concatenate(
        [lax.dot_general(mn[s].astype(BF), f2[...], NT, preferred_element_type=F32) for s in range(4)], axis=1
    )
    p_ref[...] = jnp.zeros(p_ref.shape, F32)
    p_ref[0:44] = pr[0:44]
    p_ref[64:108] = pr[44:88]
    tr = p_ref[...].T
    for h in range(2):
        for s in range(4):
            rs32[h, s * 4 : s * 4 + 4, :] = jnp.concatenate(
                [tr[s * 32 + eg * 4 : s * 32 + eg * 4 + 4, h * 64 : h * 64 + 48] for eg in range(8)], axis=1
            )
    rs[...] = rs32[...].astype(BF)
    pl.semaphore_wait(sem, N - 1)

    own = at(col * 16, 16, 16)
    pltpu.make_async_copy(ls, lmsg.at[own], l_recv).start()
    pltpu.make_async_copy(rs, rt.at[row], r1_recv).start()

    def send_right(s, _):
        pltpu.make_async_remote_copy(
            src_ref=rs, dst_ref=rt.at[row], send_sem=r1_send, recv_sem=r1_recv,
            device_id=(lax.rem(row + s, ROWS), col), device_id_type=MESH,
        ).start()
        return 0

    lax.fori_loop(1, ROWS, send_right, 0)

    def send_left(s, _):
        pltpu.make_async_remote_copy(
            src_ref=ls, dst_ref=lmsg.at[own], send_sem=l_send, recv_sem=l_recv,
            device_id=(row, lax.rem(col + s, COLS)), device_id_type=MESH,
        ).start()
        return 0

    lax.fori_loop(1, COLS, send_left, 0)

    wof[...] = wo[...].astype(F32)
    bd[...] = jnp.zeros(bd.shape, BF)

    def place(b, _):
        w = wof[pl.ds((b % 8) * 4 + b // 8, 32, stride=32), :].astype(BF)
        for q in range(4):
            bd[at(b * 128 + q * 32, 32, 32), q * 128 : q * 128 + 128] = w
        return 0

    lax.fori_loop(0, 32, place, 0, unroll=4)
    pltpu.make_async_copy(rt, rt, r1_recv).wait()
    own_half = pltpu.make_async_copy(rt.at[col // 2, col % 2], rmsg.at[own], r2_recv)
    own_half.start()

    def forward_right(s, _):
        t = lax.rem(col + s, COLS)
        pltpu.make_async_remote_copy(
            src_ref=rt.at[lax.div(t, 2), lax.rem(t, 2)], dst_ref=rmsg.at[own], send_sem=r2_send, recv_sem=r2_recv,
            device_id=(row, t), device_id_type=MESH,
        ).start()
        return 0

    lax.fori_loop(1, COLS, forward_right, 0)
    psf[...] = ps[...].reshape(CJ * RI, 128).astype(F32)
    wedge[0:256] = wl[...].T
    wedge[256:512] = wr[...].T
    pltpu.make_async_copy(rmsg, rmsg, r2_recv).wait()
    pltpu.make_async_copy(lmsg, lmsg, l_recv).wait()

    rmt[...] = rmsg[...].T

    def outer(u, _):
        a, b = iota((256, 256), 0), iota((256, 256), 1)
        for w in range(4):
            pick = ones_where((a // 4 == b // 4) & (a % 4 == w) & (b % 4 == u))
            sel = jnp.dot(rmt[...], pick, preferred_element_type=F32).astype(BF)
            x = jnp.dot(sel, lmsg[...], preferred_element_type=F32) * (1.0 / 64)
            for eg in range(8):
                for qt in range(6):
                    lhs[
                        at(qt // 3 * 576 + u * 144 + qt % 3 * 48, 48, 16),
                        w * 1024 + eg * 128 : w * 1024 + eg * 128 + 128,
                    ] = x[eg * 48 : eg * 48 + 48, qt * 128 : qt * 128 + 128].astype(BF)
        return 0

    lax.fori_loop(0, 4, outer, 0)

    def cells_of(half):
        rows = at(((col // 2) * 8 + row) * 16, 16, 16)
        return lh.at[2 * half : 2 * half + 2, rows, at(col % 2 * 128, 128, 128)]

    def scatter(half, o):
        z_row = [lax.rem(row + o + d, 4) for d in range(4)]
        k = lax.rem(col + lax.div(o, 4), 2)
        for b in range(4):
            for a in range(4):
                r = y_row[(a + b) % 4] + z_row[a]
                c = x_col[a] + y_col[(a + b) % 4] + k

                def start(r=r, c=c):
                    pltpu.make_async_remote_copy(
                        src_ref=send.at[r * COLS + c, 2 * half : 2 * half + 2], dst_ref=cells_of(half),
                        send_sem=e_send.at[half], recv_sem=e_recv.at[half], device_id=(r, c), device_id_type=MESH,
                    ).start()

                if a or b:
                    start()
                else:
                    pl.when(o > 0)(start)

    for half in range(2):
        lo, hi = (0, 6) if half == 0 else (6, 11)

        def project(u, _, half=half):
            if half:
                scatter(0, 2 * u)
                scatter(0, 2 * u + 1)
            rows = at(half * 576 + u * 288, 288, 16)
            osc[at(u * 288, 288, 16), :] = jnp.dot(lhs[rows, :], bd[...], preferred_element_type=F32)
            return 0

        lax.fori_loop(0, 2, project, 0)

        def normalize(ia, _, lo=lo, hi=hi, half=half):
            if half:
                pl.when(lax.rem(ia, 2) == 0)(lambda: scatter(0, 4 + lax.div(ia, 2)))
            for ib in range(lo, hi):
                g, u = slot(ia, ib)
                g = g - 12 * half
                upd = osc[at(u * 144 + g // 4 * 48, 48, 8), at(g % 4 * 128, 128, 128)][:44]
                cells = pl.ds(44 * (ia // 4) + in_half(ia % 4, ib), CJ, stride=RI)
                m = psf[cells, :] + upd
                psf[cells, :] = m
                c = m - jnp.mean(m, axis=-1, keepdims=True)
                n = c * lax.rsqrt(jnp.mean(c * c, axis=-1, keepdims=True) + 1e-05)
                pn[ia, 44 * ib : 44 * ib + 44] = n
            if half:
                pn[ia, 484:512] = jnp.zeros((28, 128), F32)
            p = pn[ia, half * 256 : half * 256 + 256].astype(BF)
            proj = lax.dot_general(wedge[...], p, NT, preferred_element_type=F32)
            left = sigmoid(proj[0:128]) * proj[128:256]
            right = sigmoid(proj[256:384]) * proj[384:512]
            rows = at(ia * PITCH, 128, 8)
            for t in range(2):
                el[t, rows, :] = left[:, t * 128 : t * 128 + 128]
                er[t, rows, :] = right[:, t * 128 : t * 128 + 128]
            return 0

        lax.fori_loop(0, 8, normalize, 0)

        def pack(c, _, half=half):
            for t in range(2):
                cells = pl.ds(c, 8, stride=PITCH)
                send[c, 2 * half + t] = jnp.concatenate([el[t, cells, :], er[t, cells, :]], axis=0).astype(BF)
            return 0

        lax.fori_loop(0, N, pack, 0, unroll=8)
        pltpu.make_async_copy(send.at[me, 2 * half : 2 * half + 2], cells_of(half), e_recv.at[half]).start()

    def scatter_all(o, _):
        scatter(1, o)
        return 0

    lax.fori_loop(0, 8, scatter_all, 0)

    for t in range(4):
        lo, hi = SPAN[t]
        for b in range(lo, hi):
            f, n = iota((256, 128), 0), iota((256, 128), 1)
            k = n % 64
            hit = (f // 128 == n // 64) & (f % 128 + 128 * t == 44 * b + k) & (k < 44)
            sw[t, :, (b - lo) * 128 : (b - lo) * 128 + 128] = ones_where(hit)
            n, f = iota((128, 256), 0), iota((128, 256), 1)
            k = n % 16
            j = jnp.where(k < 6, 6 * (n % 64 // 16) + k, 5 * (n % 64 // 16) + k + 18)
            hit = (f // 128 == n // 64) & (f % 128 + 128 * t == 44 * b + j) & (k < 11)
            s2[t, (b - lo) * 128 : (b - lo) * 128 + 128, :] = ones_where(hit)
    rop32[...] = jnp.zeros(rop32.shape, F32)

    def gates(ia, _):
        gate[ia] = sigmoid(jnp.dot(pn[ia].astype(BF), wg[...], preferred_element_type=F32))
        return 0

    lax.fori_loop(0, 8, gates, 0)

    for half in range(2):
        part = lh.at[2 * half : 2 * half + 2]
        pltpu.make_async_copy(part, part, e_recv.at[half]).wait()

    def widen(m, _):
        ys = []
        for t in range(4):
            lo, hi = SPAN[t]
            ys.append(
                jnp.dot(lh[t, at(m * 256, 256, 256), :], sw[t, :, : (hi - lo) * 128], preferred_element_type=F32)
            )
        for b in range(11):
            x = None
            for t in range(4):
                lo, hi = SPAN[t]
                if lo <= b < hi:
                    y = ys[t][:, (b - lo) * 128 : (b - lo) * 128 + 128]
                    x = y if x is None else x + y
            x = x.reshape(2, 8, 2, 8, 128)
            for q in range(2):
                p = 2 * m + q
                lop[b * 64 : b * 64 + 64, at(p * 128, 128, 128)] = x[q, :, 0].reshape(64, 128).astype(BF)
                for r in range(8):
                    rop32[p, pl.ds(r * 128 + b, 8, stride=16), :] = x[q, r, 1]
        return 0

    lax.fori_loop(0, 4, widen, 0)
    for p in range(8):
        rop[:, p * 128 : p * 128 + 128] = rop32[p].astype(BF)

    y0 = col // 2 % 2

    def product(step, _):
        odd, flip = step % 2, step // 2
        pairs = (
            2 * lax.rem(x + 2 - odd, 4) + (y0 + flip) % 2,
            2 * lax.rem(x + 3 * odd, 4) + (y0 + 1 + flip) % 2,
        )
        keys = jnp.concatenate([rop[at(p * 128, 128, 128), :] for p in pairs], axis=0)
        c = lax.dot_general(lop[...], keys, NT, preferred_element_type=F32).astype(BF)
        for q in range(2):
            for b in range(11):
                lhs2[q * 64 : q * 64 + 64, b * 128 : b * 128 + 128] = c[b * 64 : b * 64 + 64, q * 128 : q * 128 + 128]
        zs = []
        for t in range(4):
            lo, hi = SPAN[t]
            z = jnp.dot(lhs2[:, lo * 128 : hi * 128], s2[t, : (hi - lo) * 128, :], preferred_element_type=F32)
            zs.append(z.reshape(16, 8, 256))
        for h in range(2):
            z = jnp.concatenate([zs[2 * h], zs[2 * h + 1]], axis=1).astype(BF)
            for q in range(2):
                sb[h, at(pairs[q] * 8, 8, 8)] = z[8 * q : 8 * q + 8]

        for dr in range(ROWS):
            r = lax.rem(row + dr, ROWS)
            for k in range(2):
                for p in pairs:

                    def start(r=r, k=k, p=p):
                        pltpu.make_async_remote_copy(
                            src_ref=sb.at[:, p * 8 + r, :, k * 128 : k * 128 + 128], dst_ref=rv.at[me],
                            send_sem=c_send, recv_sem=c_recv, device_id=(r, 2 * p + k), device_id_type=MESH,
                        ).start()

                    if dr:
                        start()
                    else:
                        pl.when(2 * p + k != col)(start)
        return 0

    lax.fori_loop(0, 4, product, 0)
    back = sb.at[:, col // 2 * 8 + row, :, at(col % 2 * 128, 128, 128)]
    pltpu.make_async_copy(back, rv.at[me], c_recv).start()
    pltpu.make_async_copy(rv, rv, c_recv).wait()

    def unpack(c, _):
        for h in range(2):
            rc[h, at(c * PITCH2, 16, 8), :] = rv[c, h].astype(F32)
        return 0

    lax.fori_loop(0, N, unpack, 0, unroll=8)

    def finish(ia, _):
        for t in range(4):
            z = rc[t // 2, pl.ds(t % 2 * 8 + ia, 128, stride=PITCH2), :]
            c = z - jnp.mean(z, axis=0, keepdims=True)
            n = (c * lax.rsqrt(jnp.mean(c * c, axis=0, keepdims=True) + 1e-05)).astype(BF)
            branch = lax.dot_general(n, wout[...], TN, preferred_element_type=F32)
            br[t * 128 : t * 128 + 128] = branch * gate[ia, t * 128 : t * 128 + 128]
        for ib in range(11):
            cells = pl.ds(44 * (ia // 4) + in_half(ia % 4, ib), CJ, stride=RI)
            psf[cells, :] = psf[cells, :] + br[44 * ib : 44 * ib + 44]
        return 0

    lax.fori_loop(0, 8, finish, 0)
    out[...] = psf[...].astype(BF).reshape(CJ, RI, 128)

    def sent(src, sem):
        pltpu.make_async_remote_copy(
            src_ref=src, dst_ref=src, send_sem=sem, recv_sem=l_recv, device_id=dev((me + 1) % N), device_id_type=MESH
        ).wait_send()

    sent(lmsg.at[0:240], l_send)
    sent(rt.at[0:7], r1_send)
    sent(rmsg.at[0:240], r2_send)
    for half in range(2):
        sent(send.at[0 : N - 1, 0:2], e_send.at[half])
    sent(rv.at[0 : N - 1], c_send)


def per_device(hf, ps, f1, f2, wo, wl, wr, wg, wout):
    dma = pltpu.SemaphoreType.DMA
    vm = pltpu.VMEM
    out = pl.pallas_call(
        kernel,
        out_shape=jax.ShapeDtypeStruct((CJ, RI, 128), BF),
        in_specs=[VM] * 9,
        out_specs=VM,
        scratch_shapes=[
            vm((96, 1024), F32), vm((128, 128), F32), vm((16, 768), BF), vm((2, 16, 384), F32), vm((2, 16, 384), BF),
            vm((256, 768), BF), vm((8, 2, 16, 384), BF), vm((256, 384), BF), vm((384, 256), BF), vm((1024, 128), F32),
            vm((4096, 512), BF), vm((1152, 4096), BF), vm((576, 512), F32), vm((CJ * RI, 128), F32),
            vm((8, 512, 128), F32), vm((2, 8 * PITCH, 128), F32), vm((2, 8 * PITCH, 128), F32), vm((512, 128), BF),
            vm((8, 512, 128), F32), vm((N, 4, 16, 128), BF), vm((4, 1024, 256), BF), vm((4, 256, 512), BF),
            vm((4, 512, 256), BF), vm((704, 1024), BF), vm((8, 1024, 128), F32), vm((1024, 1024), BF),
            vm((128, 1408), BF), vm((2, 64, 16, 256), BF), vm((N, 2, 16, 128), BF), vm((2, N * PITCH2, 128), F32),
            vm((512, 128), F32),
            dma, dma, dma, dma, dma, dma, dma((2,)), dma((2,)), dma, dma,
        ],
        compiler_params=pltpu.CompilerParams(
            vmem_limit_bytes=60 * 2**20, collective_id=0, has_side_effects=True
        ),
    )(hf, ps.transpose(1, 0, 2), f1.T, f2.T, wo, wl, wr, wg, wout)
    return out.transpose(1, 0, 2)


def solution(mesh):
    return jax.shard_map(
        per_device,
        mesh=mesh,
        in_specs=(P("col", "row", None), P("row", "col", None), P(), P(), P(), P(), P(), P(), P()),
        out_specs=P("row", "col", None),
        check_vma=False,
    )
```

```python
import jax
import jax.numpy as jnp
from jax import lax
from jax.experimental import pallas as pl
from jax.experimental.pallas import tpu as pltpu
from jax.sharding import PartitionSpec as P

ROWS, COLS = 8, 16
N = ROWS * COLS
RI, CJ = 88, 44
PITCH, PITCH2 = 136, 24
MESH = pl.DeviceIdType.MESH
VM = pl.BlockSpec(memory_space=pltpu.VMEM)
F32, BF = jnp.float32, jnp.bfloat16
NT = (((1,), (1,)), ((), ()))
TN = (((0,), (0,)), ((), ()))
PARTS = ((0, 6, 0, 2), (6, 11, 2, 4))
SPAN = ((0, 3), (2, 6), (5, 9), (8, 11))


def in_half(a, b):
    return 6 * a + b if b < 6 else 24 + 5 * a + b - 6


def slot(a, b, h):
    i = in_half(a, b) - (0 if b < 6 else 24)
    return lax.div(i, 4) + h * (6 if b < 6 else 5), lax.rem(i, 4)


def group_rows(g):
    return 4 * (g if g < 6 else g + 5 if g < 12 else g - 6 if g < 17 else g)


def dev(flat):
    return (flat // COLS, flat % COLS)


def sigmoid(v):
    return 0.5 * jnp.tanh(0.5 * v) + 0.5


def iota(shape, dim):
    return lax.broadcasted_iota(jnp.int32, shape, dim)


def ones_where(mask):
    return mask.astype(F32).astype(BF)


def at(start, size, align):
    return pl.ds(pl.multiple_of(start, align), size)


def kernel(
    hf, ps, f1, f2, wo, wl, wr, wg, wout, out,
    a_ref, p_ref, ls, rs32, rs, lmsg, rt, rmsg, rmt, wof, bd, lhs, osc, rsel, psf, pn, el, er, wedge, gate,
    send, lh, sw, s2, lop, rop32, rop, lhs2, sb, rv, rc, br, psb,
    p_load, l2_send, l2_recv, l_send, l_recv, r1_send, r1_recv, r2_send, r2_recv, e_send, e_recv, c_send, c_recv,
):
    row, col = lax.axis_index("row"), lax.axis_index("col")
    me = row * COLS + col
    around = [lax.rem(col + c, COLS) for c in range(COLS)]
    x, y = col // 4, row // 4 * 2 + col // 2 % 2
    x_col = [lax.rem(x + d, 4) * 4 for d in range(4)]
    y_col = [lax.rem(lax.rem(y + d, 4), 2) * 2 for d in range(4)]
    y_row = [lax.div(lax.rem(y + d, 4), 2) * 4 for d in range(4)]
    sem = pltpu.get_barrier_semaphore()

    for c in range(1, COLS):
        pl.semaphore_signal(sem, inc=1, device_id=(row, around[c]), device_id_type=MESH)
    for r in range(1, ROWS):
        pl.semaphore_signal(sem, inc=1, device_id=(lax.rem(row + r, ROWS), col), device_id_type=MESH)
    load = pltpu.make_async_copy(ps, psb, p_load)
    load.start()

    v = hf[...].astype(F32)
    centered = v - jnp.mean(v, axis=-1, keepdims=True)
    mn = centered * lax.rsqrt(jnp.mean(centered * centered, axis=-1, keepdims=True) + 1e-05)
    for s in range(4):
        for g in range(22):
            qt, q = g // 4, g % 4
            a_ref[qt * 16 + s * 4 : qt * 16 + s * 4 + 4, q * 256 : q * 256 + 256] = mn[
                s, group_rows(g) : group_rows(g) + 4
            ]
    a_ref[80:96, 512:1024] = jnp.zeros((16, 512), F32)
    lm = jnp.concatenate(
        [
            lax.dot_general(a_ref[:, q * 256 : q * 256 + 256].astype(BF), f1[...], NT, preferred_element_type=F32)
            for q in range(4)
        ],
        axis=1,
    )
    for qt in range(6):
        ls[:, qt * 128 : qt * 128 + 128] = lm[qt * 16 : qt * 16 + 16].astype(BF)
    pr = jnp.concatenate(
        [lax.dot_general(mn[s].astype(BF), f2[...], NT, preferred_element_type=F32) for s in range(4)], axis=1
    )
    p_ref[...] = jnp.zeros(p_ref.shape, F32)
    p_ref[0:44] = pr[0:44]
    p_ref[64:108] = pr[44:88]
    tr = p_ref[...].T
    for h in range(2):
        for s in range(4):
            rs32[h, s * 4 : s * 4 + 4, :] = jnp.concatenate(
                [tr[s * 32 + eg * 4 : s * 32 + eg * 4 + 4, h * 64 : h * 64 + 48] for eg in range(8)], axis=1
            )
    rs[...] = rs32[...].astype(BF)
    pl.semaphore_wait(sem, COLS + ROWS - 2)

    own = at(col * 16, 16, 16)
    chip, core = lax.div(col, 2), lax.rem(col, 2)
    pltpu.make_async_copy(ls, lmsg.at[chip, core], l_recv).start()
    pltpu.make_async_copy(rs, rt.at[row], r1_recv).start()

    def send_right(s, _):
        pltpu.make_async_remote_copy(
            src_ref=rs, dst_ref=rt.at[row], send_sem=r1_send, recv_sem=r1_recv,
            device_id=(lax.rem(row + s, ROWS), col), device_id_type=MESH,
        ).start()
        return 0

    lax.fori_loop(1, ROWS, send_right, 0)

    def send_left(s, _):
        pltpu.make_async_remote_copy(
            src_ref=ls, dst_ref=lmsg.at[chip, core], send_sem=l_send, recv_sem=l_recv,
            device_id=(row, lax.rem(col + 2 * s, COLS)), device_id_type=MESH,
        ).start()
        return 0

    lax.fori_loop(1, 8, send_left, 0)

    wof[...] = wo[...].astype(F32)
    bd[...] = jnp.zeros(bd.shape, BF)

    def place(b, _):
        w = wof[pl.ds((b % 8) * 4 + b // 8, 32, stride=32), :].astype(BF)
        for q in range(4):
            bd[at(b * 128 + q * 32, 32, 32), q * 128 : q * 128 + 128] = w
        return 0

    lax.fori_loop(0, 32, place, 0, unroll=4)
    pltpu.make_async_copy(rt, rt, r1_recv).wait()
    own_half = pltpu.make_async_copy(rt.at[col // 2, col % 2], rmsg.at[own], r2_recv)
    own_half.start()

    def forward_right(s, _):
        t = lax.rem(col + s, COLS)
        pltpu.make_async_remote_copy(
            src_ref=rt.at[lax.div(t, 2), lax.rem(t, 2)], dst_ref=rmsg.at[own], send_sem=r2_send, recv_sem=r2_recv,
            device_id=(row, t), device_id_type=MESH,
        ).start()
        return 0

    lax.fori_loop(1, COLS, forward_right, 0)
    pltpu.make_async_copy(lmsg.at[:, core], lmsg.at[:, core], l_recv).wait()
    share = pltpu.make_async_remote_copy(
        src_ref=lmsg.at[:, core], dst_ref=lmsg.at[:, core], send_sem=l2_send, recv_sem=l2_recv,
        device_id=(row, col + 1 - 2 * core), device_id_type=MESH,
    )
    share.start()
    load.wait()
    psf[...] = psb[...].reshape(CJ * RI, 128).astype(F32)
    wedge[0:256] = wl[...].T
    wedge[256:512] = wr[...].T
    pltpu.make_async_copy(rmsg, rmsg, r2_recv).wait()
    rmt[...] = rmsg[...].T

    def pick(u, _):
        a, b = iota((256, 256), 0), iota((256, 256), 1)
        for w in range(4):
            hit = ones_where((a // 4 == b // 4) & (a % 4 == w) & (b % 4 == u))
            rsel[u, w * 384 : w * 384 + 384] = jnp.dot(rmt[...], hit, preferred_element_type=F32).astype(BF)
        return 0

    lax.fori_loop(0, 4, pick, 0)
    share.wait()


    def cells_of(m):
        return lh.at[PARTS[m][2] : PARTS[m][3], at((chip * 8 + row) * 16, 16, 16), at(core * 128, 128, 128)]

    def scatter(m, o):
        z_row = [lax.rem(row + o + d, 4) for d in range(4)]
        k = lax.rem(col + lax.div(o, 4), 2)
        for b in range(4):
            for a in range(4):
                r = y_row[(a + b) % 4] + z_row[a]
                c = x_col[a] + y_col[(a + b) % 4] + k

                def start(r=r, c=c):
                    pltpu.make_async_remote_copy(
                        src_ref=send.at[r * COLS + c, PARTS[m][2] : PARTS[m][3]], dst_ref=cells_of(m),
                        send_sem=e_send.at[m], recv_sem=e_recv.at[m], device_id=(r, c), device_id_type=MESH,
                    ).start()

                if a or b:
                    start()
                else:
                    pl.when(o > 0)(start)

    for m, (lo, hi, t_lo, t_hi) in enumerate(PARTS):

        def outer(u, _, m=m):
            if m:
                scatter(m - 1, u)
            for w in range(4):
                x = jnp.dot(
                    rsel[u, w * 384 : w * 384 + 384],
                    lmsg[:, :, :, m * 384 : m * 384 + 384].reshape(256, 384),
                    preferred_element_type=F32,
                ) * (1.0 / 64)
                for eg in range(8):
                    for qt in range(3):
                        lhs[at(u * 144 + qt * 48, 48, 16), w * 1024 + eg * 128 : w * 1024 + eg * 128 + 128] = x[
                            eg * 48 : eg * 48 + 48, qt * 128 : qt * 128 + 128
                        ].astype(BF)
            return 0

        lax.fori_loop(0, 4, outer, 0)

        def project(u, _):
            rows = at(u * 288, 288, 16)
            osc[rows, :] = jnp.dot(lhs[rows, :], bd[...], preferred_element_type=F32)
            return 0

        lax.fori_loop(0, 2, project, 0)

        def normalize(ia, _, m=m, lo=lo, hi=hi, t_lo=t_lo, t_hi=t_hi):
            if m:
                pl.when(lax.rem(ia, 2) == 0)(lambda: scatter(m - 1, 4 + lax.div(ia, 2)))
            h, a = lax.div(ia, 4), lax.rem(ia, 4)
            for ib in range(lo, hi):
                g, u = slot(a, ib, h)
                upd = osc[at(u * 144 + lax.div(g, 4) * 48, 48, 8), at(lax.rem(g, 4) * 128, 128, 128)][:44]
                cells = pl.ds(44 * h + in_half(a, ib), CJ, stride=RI)
                v = psf[cells, :] + upd
                psf[cells, :] = v
                c = v - jnp.mean(v, axis=-1, keepdims=True)
                n = c * lax.rsqrt(jnp.mean(c * c, axis=-1, keepdims=True) + 1e-05)
                pn[ia, 44 * ib : 44 * ib + 44] = n
            if hi == 11:
                pn[ia, 484:512] = jnp.zeros((28, 128), F32)
            p = pn[ia, t_lo * 128 : t_hi * 128].astype(BF)
            proj = lax.dot_general(wedge[...], p, NT, preferred_element_type=F32)
            left = sigmoid(proj[0:128]) * proj[128:256]
            right = sigmoid(proj[256:384]) * proj[384:512]
            rows = at(ia * PITCH, 128, 8)
            for t in range(t_hi - t_lo):
                el[t, rows, :] = left[:, t * 128 : t * 128 + 128]
                er[t, rows, :] = right[:, t * 128 : t * 128 + 128]
            return 0

        lax.fori_loop(0, 8, normalize, 0)

        def pack(c, _, t_lo=t_lo, t_hi=t_hi):
            for t in range(t_hi - t_lo):
                cells = pl.ds(c, 8, stride=PITCH)
                send[c, t_lo + t] = jnp.concatenate([el[t, cells, :], er[t, cells, :]], axis=0).astype(BF)
            return 0

        lax.fori_loop(0, N, pack, 0, unroll=8)
        pltpu.make_async_copy(send.at[me, t_lo:t_hi], cells_of(m), e_recv.at[m]).start()

    def scatter_all(o, _):
        scatter(1, o)
        return 0

    lax.fori_loop(0, 8, scatter_all, 0)

    for t in range(4):
        lo, hi = SPAN[t]
        for b in range(lo, hi):
            f, n = iota((256, 128), 0), iota((256, 128), 1)
            k = n % 64
            hit = (f // 128 == n // 64) & (f % 128 + 128 * t == 44 * b + k) & (k < 44)
            sw[t, :, (b - lo) * 128 : (b - lo) * 128 + 128] = ones_where(hit)
            n, f = iota((128, 256), 0), iota((128, 256), 1)
            k = n % 16
            a = n % 64 // 16
            j = jnp.where(k < 6, 6 * a + k, 18 + 5 * a + k)
            hit = (f // 128 == n // 64) & (f % 128 + 128 * t == 44 * b + j) & (k < 11)
            s2[t, (b - lo) * 128 : (b - lo) * 128 + 128, :] = ones_where(hit)
    rop32[...] = jnp.zeros(rop32.shape, F32)

    def gates(ia, _):
        gate[ia] = sigmoid(jnp.dot(pn[ia].astype(BF), wg[...], preferred_element_type=F32))
        return 0

    lax.fori_loop(0, 8, gates, 0)

    for m, (_, _, t_lo, t_hi) in enumerate(PARTS):
        part = lh.at[t_lo:t_hi]
        pltpu.make_async_copy(part, part, e_recv.at[m]).wait()

    def widen(m, _):
        ys = []
        for t in range(4):
            lo, hi = SPAN[t]
            ys.append(
                jnp.dot(lh[t, at(m * 256, 256, 256), :], sw[t, :, : (hi - lo) * 128], preferred_element_type=F32)
            )
        for b in range(11):
            x = None
            for t in range(4):
                lo, hi = SPAN[t]
                if lo <= b < hi:
                    y = ys[t][:, (b - lo) * 128 : (b - lo) * 128 + 128]
                    x = y if x is None else x + y
            x = x.reshape(2, 8, 2, 8, 128)
            for q in range(2):
                p = 2 * m + q
                lop[b * 64 : b * 64 + 64, at(p * 128, 128, 128)] = x[q, :, 0].reshape(64, 128).astype(BF)
                for r in range(8):
                    rop32[p, pl.ds(r * 128 + b, 8, stride=16), :] = x[q, r, 1]
        return 0

    lax.fori_loop(0, 4, widen, 0)
    for p in range(8):
        rop[:, p * 128 : p * 128 + 128] = rop32[p].astype(BF)

    y0 = col // 2 % 2

    def product(step, _):
        odd, flip = step % 2, step // 2
        pairs = (
            2 * lax.rem(x + 2 - odd, 4) + (y0 + flip) % 2,
            2 * lax.rem(x + 3 * odd, 4) + (y0 + 1 + flip) % 2,
        )
        keys = jnp.concatenate([rop[at(p * 128, 128, 128), :] for p in pairs], axis=0)
        c = lax.dot_general(lop[...], keys, NT, preferred_element_type=F32).astype(BF)
        for q in range(2):
            for b in range(11):
                lhs2[q * 64 : q * 64 + 64, b * 128 : b * 128 + 128] = c[b * 64 : b * 64 + 64, q * 128 : q * 128 + 128]
        zs = []
        for t in range(4):
            lo, hi = SPAN[t]
            z = jnp.dot(lhs2[:, lo * 128 : hi * 128], s2[t, : (hi - lo) * 128, :], preferred_element_type=F32)
            zs.append(z.reshape(16, 8, 256))
        for h in range(2):
            z = jnp.concatenate([zs[2 * h], zs[2 * h + 1]], axis=1).astype(BF)
            for q in range(2):
                sb[h, at(pairs[q] * 8, 8, 8)] = z[8 * q : 8 * q + 8]

        for dr in range(ROWS):
            r = lax.rem(row + dr, ROWS)
            for k in range(2):
                for p in pairs:

                    def start(r=r, k=k, p=p):
                        pltpu.make_async_remote_copy(
                            src_ref=sb.at[:, p * 8 + r, :, k * 128 : k * 128 + 128], dst_ref=rv.at[me],
                            send_sem=c_send, recv_sem=c_recv, device_id=(r, 2 * p + k), device_id_type=MESH,
                        ).start()

                    if dr:
                        start()
                    else:
                        pl.when(2 * p + k != col)(start)
        return 0

    lax.fori_loop(0, 4, product, 0)
    back = sb.at[:, col // 2 * 8 + row, :, at(col % 2 * 128, 128, 128)]
    pltpu.make_async_copy(back, rv.at[me], c_recv).start()
    pltpu.make_async_copy(rv, rv, c_recv).wait()

    def unpack(c, _):
        for h in range(2):
            rc[h, at(c * PITCH2, 16, 8), :] = rv[c, h].astype(F32)
        return 0

    lax.fori_loop(0, N, unpack, 0, unroll=8)

    def finish(ia, _):
        for t in range(4):
            z = rc[t // 2, pl.ds(t % 2 * 8 + ia, 128, stride=PITCH2), :]
            c = z - jnp.mean(z, axis=0, keepdims=True)
            n = (c * lax.rsqrt(jnp.mean(c * c, axis=0, keepdims=True) + 1e-05)).astype(BF)
            branch = lax.dot_general(n, wout[...], TN, preferred_element_type=F32)
            br[t * 128 : t * 128 + 128] = branch * gate[ia, t * 128 : t * 128 + 128]
        for ib in range(11):
            cells = pl.ds(44 * lax.div(ia, 4) + in_half(lax.rem(ia, 4), ib), CJ, stride=RI)
            psf[cells, :] = psf[cells, :] + br[44 * ib : 44 * ib + 44]
        return 0

    lax.fori_loop(0, 8, finish, 0)
    out[...] = psf[...].astype(BF).reshape(CJ, RI, 128)

    def sent(src, sem):
        pltpu.make_async_remote_copy(
            src_ref=src, dst_ref=src, send_sem=sem, recv_sem=l_recv, device_id=dev((me + 1) % N), device_id_type=MESH
        ).wait_send()

    sent(lmsg.at[0:7, 0], l_send)
    sent(rt.at[0:7], r1_send)
    sent(rmsg.at[0:240], r2_send)
    for m, (_, _, t_lo, t_hi) in enumerate(PARTS):
        sent(send.at[0 : N - 1, t_lo:t_hi], e_send.at[m])
    sent(rv.at[0 : N - 1], c_send)


def per_device(hf, ps, f1, f2, wo, wl, wr, wg, wout):
    dma = pltpu.SemaphoreType.DMA
    vm = pltpu.VMEM
    out = pl.pallas_call(
        kernel,
        out_shape=jax.ShapeDtypeStruct((CJ, RI, 128), BF),
        in_specs=[VM, pl.BlockSpec(memory_space=pl.ANY)] + [VM] * 7,
        out_specs=VM,
        scratch_shapes=[
            vm((96, 1024), F32), vm((128, 128), F32), vm((16, 768), BF), vm((2, 16, 384), F32), vm((2, 16, 384), BF),
            vm((8, 2, 16, 768), BF), vm((8, 2, 16, 384), BF), vm((256, 384), BF), vm((384, 256), BF), vm((1024, 128), F32),
            vm((4096, 512), BF), vm((576, 4096), BF), vm((576, 512), F32), vm((4, 1536, 256), BF), vm((CJ * RI, 128), F32),
            vm((8, 512, 128), F32), vm((2, 8 * PITCH, 128), F32), vm((2, 8 * PITCH, 128), F32), vm((512, 128), BF),
            vm((8, 512, 128), F32), vm((N, 4, 16, 128), BF), vm((4, 1024, 256), BF), vm((4, 256, 512), BF),
            vm((4, 512, 256), BF), vm((704, 1024), BF), vm((8, 1024, 128), F32), vm((1024, 1024), BF),
            vm((128, 1408), BF), vm((2, 64, 16, 256), BF), vm((N, 2, 16, 128), BF), vm((2, N * PITCH2, 128), F32),
            vm((512, 128), F32), vm((CJ, RI, 128), BF),
            dma, dma, dma, dma, dma, dma, dma, dma, dma, dma((2,)), dma((2,)), dma, dma,
        ],
        compiler_params=pltpu.CompilerParams(
            vmem_limit_bytes=60 * 2**20, collective_id=0, has_side_effects=True
        ),
    )(hf, ps.transpose(1, 0, 2), f1.T, f2.T, wo, wl, wr, wg, wout)
    return out.transpose(1, 0, 2)


def solution(mesh):
    return jax.shard_map(
        per_device,
        mesh=mesh,
        in_specs=(P("col", "row", None), P("row", "col", None), P(), P(), P(), P(), P(), P(), P()),
        out_specs=P("row", "col", None),
        check_vma=False,
    )
```

```python
import jax
import jax.numpy as jnp
from jax import lax
from jax.experimental import pallas as pl
from jax.experimental.pallas import tpu as pltpu
from jax.sharding import PartitionSpec as P

ROWS, COLS = 8, 16
N = ROWS * COLS
RI, CJ = 88, 44
PITCH, PITCH2 = 136, 24
MESH = pl.DeviceIdType.MESH
VM = pl.BlockSpec(memory_space=pltpu.VMEM)
F32, BF = jnp.float32, jnp.bfloat16
NT = (((1,), (1,)), ((), ()))
TN = (((0,), (0,)), ((), ()))
PARTS = ((0, 6, 0, 2), (6, 11, 2, 4))
SPAN = ((0, 3), (2, 6), (5, 9), (8, 11))


def in_half(a, b):
    return 6 * a + b if b < 6 else 24 + 5 * a + b - 6


def slot(a, b, h):
    i = in_half(a, b) - (0 if b < 6 else 24)
    return lax.div(i, 4) + h * (6 if b < 6 else 5), lax.rem(i, 4)


def group_rows(g):
    return 4 * (g if g < 6 else g + 5 if g < 12 else g - 6 if g < 17 else g)


def dev(flat):
    return (flat // COLS, flat % COLS)


def sigmoid(v):
    return 0.5 * jnp.tanh(0.5 * v) + 0.5


def iota(shape, dim):
    return lax.broadcasted_iota(jnp.int32, shape, dim)


def ones_where(mask):
    return mask.astype(F32).astype(BF)


def at(start, size, align):
    return pl.ds(pl.multiple_of(start, align), size)


def kernel(
    hf, ps, f1, f2, wo, wl, wr, wg, wout, out,
    a_ref, p_ref, ls, rs32, rs, lmsg, rt, rmsg, rmt, wof, bd, lhs, osc, rsel, psf, pn, el, er, wedge, gate,
    send, lh, sw, s2, lop, rop32, rop, lhs2, sb, rv, rc, br, psb,
    p_load, l2_send, l2_recv, l_send, l_recv, r1_send, r1_recv, r2_send, r2_recv, e_send, e_recv, c_send, c_recv,
):
    row, col = lax.axis_index("row"), lax.axis_index("col")
    me = row * COLS + col
    around = [lax.rem(col + c, COLS) for c in range(COLS)]
    x, y = col // 4, row // 4 * 2 + col // 2 % 2
    x_col = [lax.rem(x + d, 4) * 4 for d in range(4)]
    y_col = [lax.rem(lax.rem(y + d, 4), 2) * 2 for d in range(4)]
    y_row = [lax.div(lax.rem(y + d, 4), 2) * 4 for d in range(4)]
    sem = pltpu.get_barrier_semaphore()

    for c in range(1, COLS):
        pl.semaphore_signal(sem, inc=1, device_id=(row, around[c]), device_id_type=MESH)
    for r in range(1, ROWS):
        pl.semaphore_signal(sem, inc=1, device_id=(lax.rem(row + r, ROWS), col), device_id_type=MESH)
    load = pltpu.make_async_copy(ps, psb, p_load)
    load.start()

    v = hf[...].astype(F32)
    centered = v - jnp.mean(v, axis=-1, keepdims=True)
    mn = centered * lax.rsqrt(jnp.mean(centered * centered, axis=-1, keepdims=True) + 1e-05)
    for s in range(4):
        for g in range(22):
            qt, q = g // 4, g % 4
            a_ref[qt * 16 + s * 4 : qt * 16 + s * 4 + 4, q * 256 : q * 256 + 256] = mn[
                s, group_rows(g) : group_rows(g) + 4
            ]
    a_ref[80:96, 512:1024] = jnp.zeros((16, 512), F32)
    lm = jnp.concatenate(
        [
            lax.dot_general(a_ref[:, q * 256 : q * 256 + 256].astype(BF), f1[...], NT, preferred_element_type=F32)
            for q in range(4)
        ],
        axis=1,
    )
    for qt in range(6):
        ls[:, qt * 128 : qt * 128 + 128] = lm[qt * 16 : qt * 16 + 16].astype(BF)
    pr = jnp.concatenate(
        [lax.dot_general(mn[s].astype(BF), f2[...], NT, preferred_element_type=F32) for s in range(4)], axis=1
    )
    p_ref[...] = jnp.zeros(p_ref.shape, F32)
    p_ref[0:44] = pr[0:44]
    p_ref[64:108] = pr[44:88]
    tr = p_ref[...].T
    for h in range(2):
        for s in range(4):
            rs32[h, s * 4 : s * 4 + 4, :] = jnp.concatenate(
                [tr[s * 32 + eg * 4 : s * 32 + eg * 4 + 4, h * 64 : h * 64 + 48] for eg in range(8)], axis=1
            )
    rs[...] = rs32[...].astype(BF)
    pl.semaphore_wait(sem, COLS + ROWS - 2)

    own = at(col * 16, 16, 16)
    chip, core = lax.div(col, 2), lax.rem(col, 2)
    pltpu.make_async_copy(ls, lmsg.at[chip, core], l_recv).start()
    pltpu.make_async_copy(rs, rt.at[row], r1_recv).start()

    def send_right(s, _):
        pltpu.make_async_remote_copy(
            src_ref=rs, dst_ref=rt.at[row], send_sem=r1_send, recv_sem=r1_recv,
            device_id=(lax.rem(row + s, ROWS), col), device_id_type=MESH,
        ).start()
        return 0

    lax.fori_loop(1, ROWS, send_right, 0)

    def send_left(s, _):
        pltpu.make_async_remote_copy(
            src_ref=ls, dst_ref=lmsg.at[chip, core], send_sem=l_send, recv_sem=l_recv,
            device_id=(row, lax.rem(col + 2 * s, COLS)), device_id_type=MESH,
        ).start()
        return 0

    lax.fori_loop(1, 8, send_left, 0)

    wof[...] = wo[...].astype(F32)
    bd[...] = jnp.zeros(bd.shape, BF)

    def place(b, _):
        w = wof[pl.ds((b % 8) * 4 + b // 8, 32, stride=32), :].astype(BF)
        for q in range(4):
            bd[at(b * 128 + q * 32, 32, 32), q * 128 : q * 128 + 128] = w
        return 0

    lax.fori_loop(0, 32, place, 0, unroll=4)
    pltpu.make_async_copy(rt, rt, r1_recv).wait()
    own_half = pltpu.make_async_copy(rt.at[col // 2, col % 2], rmsg.at[own], r2_recv)
    own_half.start()

    def forward_right(s, _):
        t = lax.rem(col + s, COLS)
        pltpu.make_async_remote_copy(
            src_ref=rt.at[lax.div(t, 2), lax.rem(t, 2)], dst_ref=rmsg.at[own], send_sem=r2_send, recv_sem=r2_recv,
            device_id=(row, t), device_id_type=MESH,
        ).start()
        return 0

    lax.fori_loop(1, COLS, forward_right, 0)
    pltpu.make_async_copy(lmsg.at[:, core], lmsg.at[:, core], l_recv).wait()
    share = pltpu.make_async_remote_copy(
        src_ref=lmsg.at[:, core], dst_ref=lmsg.at[:, core], send_sem=l2_send, recv_sem=l2_recv,
        device_id=(row, col + 1 - 2 * core), device_id_type=MESH,
    )
    share.start()
    load.wait()
    psf[...] = psb[...].reshape(CJ * RI, 128).astype(F32)
    wedge[0:256] = wl[...].T
    wedge[256:512] = wr[...].T
    pltpu.make_async_copy(rmsg, rmsg, r2_recv).wait()
    rmt[...] = rmsg[...].T

    def pick(u, _):
        a, b = iota((256, 256), 0), iota((256, 256), 1)
        for w in range(4):
            hit = ones_where((a // 4 == b // 4) & (a % 4 == w) & (b % 4 == u))
            rsel[u, w * 384 : w * 384 + 384] = jnp.dot(rmt[...], hit, preferred_element_type=F32).astype(BF)
        return 0

    lax.fori_loop(0, 4, pick, 0)
    share.wait()


    def cells_of(m):
        return lh.at[PARTS[m][2] : PARTS[m][3], at((chip * 8 + row) * 16, 16, 16), at(core * 128, 128, 128)]

    def scatter(m, o):
        z_row = [lax.rem(row + o + d, 4) for d in range(4)]
        k = lax.rem(col + lax.div(o, 4), 2)
        for b in range(4):
            for a in range(4):
                r = y_row[(a + b) % 4] + z_row[a]
                c = x_col[a] + y_col[(a + b) % 4] + k

                def start(r=r, c=c):
                    pltpu.make_async_remote_copy(
                        src_ref=send.at[r * COLS + c, PARTS[m][2] : PARTS[m][3]], dst_ref=cells_of(m),
                        send_sem=e_send.at[m], recv_sem=e_recv.at[m], device_id=(r, c), device_id_type=MESH,
                    ).start()

                if a or b:
                    start()
                else:
                    pl.when(o > 0)(start)

    for m, (lo, hi, t_lo, t_hi) in enumerate(PARTS):

        def outer(u, _, m=m):
            if m:
                scatter(m - 1, u)
            for w in range(4):
                x = jnp.dot(
                    rsel[u, w * 384 : w * 384 + 384],
                    lmsg[:, :, :, m * 384 : m * 384 + 384].reshape(256, 384),
                    preferred_element_type=F32,
                ) * (1.0 / 64)
                for eg in range(8):
                    for qt in range(3):
                        lhs[at(u * 144 + qt * 48, 48, 16), w * 1024 + eg * 128 : w * 1024 + eg * 128 + 128] = x[
                            eg * 48 : eg * 48 + 48, qt * 128 : qt * 128 + 128
                        ].astype(BF)
            return 0

        lax.fori_loop(0, 4, outer, 0)

        def project(u, _):
            rows = at(u * 288, 288, 16)
            osc[rows, :] = jnp.dot(lhs[rows, :], bd[...], preferred_element_type=F32)
            return 0

        lax.fori_loop(0, 2, project, 0)

        def normalize(ia, _, m=m, lo=lo, hi=hi, t_lo=t_lo, t_hi=t_hi):
            if m:
                pl.when(lax.rem(ia, 2) == 0)(lambda: scatter(m - 1, 4 + lax.div(ia, 2)))
            h, a = lax.div(ia, 4), lax.rem(ia, 4)
            for ib in range(lo, hi):
                g, u = slot(a, ib, h)
                upd = osc[at(u * 144 + lax.div(g, 4) * 48, 48, 8), at(lax.rem(g, 4) * 128, 128, 128)][:44]
                cells = pl.ds(44 * h + in_half(a, ib), CJ, stride=RI)
                v = psf[cells, :] + upd
                psf[cells, :] = v
                c = v - jnp.mean(v, axis=-1, keepdims=True)
                n = c * lax.rsqrt(jnp.mean(c * c, axis=-1, keepdims=True) + 1e-05)
                pn[ia, 44 * ib : 44 * ib + 44] = n
            if hi == 11:
                pn[ia, 484:512] = jnp.zeros((28, 128), F32)
            p = pn[ia, t_lo * 128 : t_hi * 128].astype(BF)
            proj = lax.dot_general(wedge[...], p, NT, preferred_element_type=F32)
            left = sigmoid(proj[0:128]) * proj[128:256]
            right = sigmoid(proj[256:384]) * proj[384:512]
            rows = at(ia * PITCH, 128, 8)
            for t in range(t_hi - t_lo):
                el[t, rows, :] = left[:, t * 128 : t * 128 + 128]
                er[t, rows, :] = right[:, t * 128 : t * 128 + 128]
            return 0

        lax.fori_loop(0, 8, normalize, 0, unroll=2)

        def pack(c, _, t_lo=t_lo, t_hi=t_hi):
            for t in range(t_hi - t_lo):
                cells = pl.ds(c, 8, stride=PITCH)
                send[c, t_lo + t] = jnp.concatenate([el[t, cells, :], er[t, cells, :]], axis=0).astype(BF)
            return 0

        lax.fori_loop(0, N, pack, 0, unroll=8)
        pltpu.make_async_copy(send.at[me, t_lo:t_hi], cells_of(m), e_recv.at[m]).start()

    def scatter_all(o, _):
        scatter(1, o)
        return 0

    lax.fori_loop(0, 8, scatter_all, 0)

    for t in range(4):
        lo, hi = SPAN[t]
        for b in range(lo, hi):
            f, n = iota((256, 128), 0), iota((256, 128), 1)
            k = n % 64
            hit = (f // 128 == n // 64) & (f % 128 + 128 * t == 44 * b + k) & (k < 44)
            sw[t, :, (b - lo) * 128 : (b - lo) * 128 + 128] = ones_where(hit)
            n, f = iota((128, 256), 0), iota((128, 256), 1)
            k = n % 16
            a = n % 64 // 16
            j = jnp.where(k < 6, 6 * a + k, 18 + 5 * a + k)
            hit = (f // 128 == n // 64) & (f % 128 + 128 * t == 44 * b + j) & (k < 11)
            s2[t, (b - lo) * 128 : (b - lo) * 128 + 128, :] = ones_where(hit)
    rop32[...] = jnp.zeros(rop32.shape, F32)

    def gates(ia, _):
        gate[ia] = sigmoid(jnp.dot(pn[ia].astype(BF), wg[...], preferred_element_type=F32))
        return 0

    lax.fori_loop(0, 8, gates, 0)

    for m, (_, _, t_lo, t_hi) in enumerate(PARTS):
        part = lh.at[t_lo:t_hi]
        pltpu.make_async_copy(part, part, e_recv.at[m]).wait()

        def widen(g, _, m=m):
            lo, hi = ((0, 5), (5, 11))[m]
            xs = {}
            for t in ((0, 1), (1, 2, 3))[m]:
                first, last = max(SPAN[t][0], lo), min(SPAN[t][1], hi)
                lanes = slice((first - SPAN[t][0]) * 128, (last - SPAN[t][0]) * 128)
                y = jnp.dot(lh[t, at(g * 256, 256, 256), :], sw[t, :, lanes], preferred_element_type=F32)
                for b in range(first, last):
                    x = y[:, (b - first) * 128 : (b - first) * 128 + 128]
                    xs[b] = xs[b] + x if b in xs else x
            for b, x in xs.items():
                x = x.reshape(2, 8, 2, 8, 128)
                for q in range(2):
                    p = 2 * g + q
                    lop[b * 64 : b * 64 + 64, at(p * 128, 128, 128)] = x[q, :, 0].reshape(64, 128).astype(BF)
                    for r in range(8):
                        rop32[p, pl.ds(r * 128 + b, 8, stride=16), :] = x[q, r, 1]
            return 0

        lax.fori_loop(0, 4, widen, 0)
    for p in range(8):
        rop[:, p * 128 : p * 128 + 128] = rop32[p].astype(BF)

    y0 = col // 2 % 2

    def product(step, _):
        odd, flip = step % 2, step // 2
        pairs = (
            2 * lax.rem(x + 2 - odd, 4) + (y0 + flip) % 2,
            2 * lax.rem(x + 3 * odd, 4) + (y0 + 1 + flip) % 2,
        )
        keys = jnp.concatenate([rop[at(p * 128, 128, 128), :] for p in pairs], axis=0)
        c = lax.dot_general(lop[...], keys, NT, preferred_element_type=F32).astype(BF)
        for q in range(2):
            for b in range(11):
                lhs2[q * 64 : q * 64 + 64, b * 128 : b * 128 + 128] = c[b * 64 : b * 64 + 64, q * 128 : q * 128 + 128]
        zs = []
        for t in range(4):
            lo, hi = SPAN[t]
            z = jnp.dot(lhs2[:, lo * 128 : hi * 128], s2[t, : (hi - lo) * 128, :], preferred_element_type=F32)
            zs.append(z.reshape(16, 8, 256))
        for h in range(2):
            z = jnp.concatenate([zs[2 * h], zs[2 * h + 1]], axis=1).astype(BF)
            for q in range(2):
                sb[h, at(pairs[q] * 8, 8, 8)] = z[8 * q : 8 * q + 8]

        for dr in range(ROWS):
            r = lax.rem(row + dr, ROWS)
            for k in range(2):
                for p in pairs:

                    def start(r=r, k=k, p=p):
                        pltpu.make_async_remote_copy(
                            src_ref=sb.at[:, p * 8 + r, :, k * 128 : k * 128 + 128], dst_ref=rv.at[me],
                            send_sem=c_send, recv_sem=c_recv.at[step], device_id=(r, 2 * p + k), device_id_type=MESH,
                        ).start()

                    if dr:
                        start()
                    else:
                        pl.when(2 * p + k != col)(start)
        return 0

    lax.fori_loop(0, 4, product, 0)
    back = sb.at[:, col // 2 * 8 + row, :, at(col % 2 * 128, 128, 128)]
    pltpu.make_async_copy(back, rv.at[me], c_recv.at[2]).start()

    for step in range(4):
        odd, flip = step % 2, step // 2
        part = rv.at[0 : N // 4]
        pltpu.make_async_copy(part, part, c_recv.at[step]).wait()
        for dx, dy in ((2 - odd, flip), (3 * odd, 1 + flip)):
            p = 2 * lax.rem(x + 4 - dx, 4) + lax.rem(y0 + dy, 2)

            def unpack(r, _, p=p):
                for k in range(2):
                    c = r * COLS + 2 * p + k
                    for h in range(2):
                        rc[h, at(c * PITCH2, 16, 8), :] = rv[c, h].astype(F32)
                return 0

            lax.fori_loop(0, ROWS, unpack, 0, unroll=4)

    def finish(ia, _):
        for t in range(4):
            z = rc[t // 2, pl.ds(t % 2 * 8 + ia, 128, stride=PITCH2), :]
            c = z - jnp.mean(z, axis=0, keepdims=True)
            n = (c * lax.rsqrt(jnp.mean(c * c, axis=0, keepdims=True) + 1e-05)).astype(BF)
            branch = lax.dot_general(n, wout[...], TN, preferred_element_type=F32)
            br[t * 128 : t * 128 + 128] = branch * gate[ia, t * 128 : t * 128 + 128]
        for ib in range(11):
            cells = pl.ds(44 * lax.div(ia, 4) + in_half(lax.rem(ia, 4), ib), CJ, stride=RI)
            psf[cells, :] = psf[cells, :] + br[44 * ib : 44 * ib + 44]
        return 0

    lax.fori_loop(0, 8, finish, 0, unroll=2)
    out[...] = psf[...].astype(BF).reshape(CJ, RI, 128)

    def sent(src, sem):
        pltpu.make_async_remote_copy(
            src_ref=src, dst_ref=src, send_sem=sem, recv_sem=l_recv, device_id=dev((me + 1) % N), device_id_type=MESH
        ).wait_send()

    sent(lmsg.at[0:7, 0], l_send)
    sent(rt.at[0:7], r1_send)
    sent(rmsg.at[0:240], r2_send)
    for m, (_, _, t_lo, t_hi) in enumerate(PARTS):
        sent(send.at[0 : N - 1, t_lo:t_hi], e_send.at[m])
    sent(rv.at[0 : N - 1], c_send)


def per_device(hf, ps, f1, f2, wo, wl, wr, wg, wout):
    dma = pltpu.SemaphoreType.DMA
    vm = pltpu.VMEM
    out = pl.pallas_call(
        kernel,
        out_shape=jax.ShapeDtypeStruct((CJ, RI, 128), BF),
        in_specs=[VM, pl.BlockSpec(memory_space=pl.ANY)] + [VM] * 7,
        out_specs=VM,
        scratch_shapes=[
            vm((96, 1024), F32), vm((128, 128), F32), vm((16, 768), BF), vm((2, 16, 384), F32), vm((2, 16, 384), BF),
            vm((8, 2, 16, 768), BF), vm((8, 2, 16, 384), BF), vm((256, 384), BF), vm((384, 256), BF), vm((1024, 128), F32),
            vm((4096, 512), BF), vm((576, 4096), BF), vm((576, 512), F32), vm((4, 1536, 256), BF), vm((CJ * RI, 128), F32),
            vm((8, 512, 128), F32), vm((2, 8 * PITCH, 128), F32), vm((2, 8 * PITCH, 128), F32), vm((512, 128), BF),
            vm((8, 512, 128), F32), vm((N, 4, 16, 128), BF), vm((4, 1024, 256), BF), vm((4, 256, 512), BF),
            vm((4, 512, 256), BF), vm((704, 1024), BF), vm((8, 1024, 128), F32), vm((1024, 1024), BF),
            vm((128, 1408), BF), vm((2, 64, 16, 256), BF), vm((N, 2, 16, 128), BF), vm((2, N * PITCH2, 128), F32),
            vm((512, 128), F32), vm((CJ, RI, 128), BF),
            dma, dma, dma, dma, dma, dma, dma, dma, dma, dma((2,)), dma((2,)), dma, dma((4,)),
        ],
        compiler_params=pltpu.CompilerParams(
            vmem_limit_bytes=60 * 2**20, collective_id=0, has_side_effects=True
        ),
    )(hf, ps.transpose(1, 0, 2), f1.T, f2.T, wo, wl, wr, wg, wout)
    return out.transpose(1, 0, 2)


def solution(mesh):
    return jax.shard_map(
        per_device,
        mesh=mesh,
        in_specs=(P("col", "row", None), P("row", "col", None), P(), P(), P(), P(), P(), P(), P()),
        out_specs=P("row", "col", None),
        check_vma=False,
    )
```

```python
import jax
import jax.numpy as jnp
from jax import lax
from jax.experimental import pallas as pl
from jax.experimental.pallas import tpu as pltpu
from jax.sharding import PartitionSpec as P

ROWS, COLS = 8, 16
N = ROWS * COLS
RI, CJ = 88, 44
PITCH, PITCH2 = 136, 24
MESH = pl.DeviceIdType.MESH
VM = pl.BlockSpec(memory_space=pltpu.VMEM)
F32, BF = jnp.float32, jnp.bfloat16
NT = (((1,), (1,)), ((), ()))
TN = (((0,), (0,)), ((), ()))
PARTS = ((0, 6, 0, 2), (6, 11, 2, 4))
SPAN = ((0, 3), (2, 6), (5, 9), (8, 11))


def in_half(a, b):
    return 6 * a + b if b < 6 else 24 + 5 * a + b - 6


def slot(a, b, h):
    i = in_half(a, b) - (0 if b < 6 else 24)
    return lax.div(i, 4) + h * (6 if b < 6 else 5), lax.rem(i, 4)


def group_rows(g):
    return 4 * (g if g < 6 else g + 5 if g < 12 else g - 6 if g < 17 else g)


def dev(flat):
    return (flat // COLS, flat % COLS)


def sigmoid(v):
    return 0.5 * jnp.tanh(0.5 * v) + 0.5


def iota(shape, dim):
    return lax.broadcasted_iota(jnp.int32, shape, dim)


def ones_where(mask):
    return mask.astype(F32).astype(BF)


def at(start, size, align):
    return pl.ds(pl.multiple_of(start, align), size)


def kernel(
    hf_any, ps_any, f1_any, f2_any, wo_any, wl_any, wr_any, wg_any, wout_any, out,
    hf, ps, f1, f2, wo, wl, wr, wg, wout,
    a_ref, p_ref, ls, rs32, rs, lmsg, rt, rmsg, rmt, wof, bd, lhs, osc, rsel, psf, pn, el, er, wedge, gate,
    send, lh, sw, s2, lop, rop32, rop, lhs2, sb, rv, rc, br,
    loaded, l2_send, l2_recv, l_send, l_recv, r1_send, r1_recv, r2_send, r2_recv, e_send, e_recv, c_send, c_recv,
):
    row, col = lax.axis_index("row"), lax.axis_index("col")
    me = row * COLS + col
    around = [lax.rem(col + c, COLS) for c in range(COLS)]
    x, y = col // 4, row // 4 * 2 + col // 2 % 2
    x_col = [lax.rem(x + d, 4) * 4 for d in range(4)]
    y_col = [lax.rem(lax.rem(y + d, 4), 2) * 2 for d in range(4)]
    y_row = [lax.div(lax.rem(y + d, 4), 2) * 4 for d in range(4)]
    sem = pltpu.get_barrier_semaphore()

    loads = [
        pltpu.make_async_copy(src, dst, loaded.at[n])
        for n, (src, dst) in enumerate(
            (
                (hf_any, hf), (f2_any, f2), (f1_any, f1), (wo_any, wo), (ps_any, ps), (wl_any, wl), (wr_any, wr),
                (wg_any, wg), (wout_any, wout),
            )
        )
    ]
    for load in loads:
        load.start()

    for c in range(1, COLS):
        pl.semaphore_signal(sem, inc=1, device_id=(row, around[c]), device_id_type=MESH)
    for r in range(1, ROWS):
        pl.semaphore_signal(sem, inc=1, device_id=(lax.rem(row + r, ROWS), col), device_id_type=MESH)

    for load in loads[:3]:
        load.wait()
    v = hf[...].astype(F32)
    centered = v - jnp.mean(v, axis=-1, keepdims=True)
    mn = centered * lax.rsqrt(jnp.mean(centered * centered, axis=-1, keepdims=True) + 1e-05)
    pr = jnp.concatenate(
        [lax.dot_general(mn[s].astype(BF), f2[...], NT, preferred_element_type=F32) for s in range(4)], axis=1
    )
    p_ref[...] = jnp.zeros(p_ref.shape, F32)
    p_ref[0:44] = pr[0:44]
    p_ref[64:108] = pr[44:88]
    tr = p_ref[...].T
    for h in range(2):
        for s in range(4):
            rs32[h, s * 4 : s * 4 + 4, :] = jnp.concatenate(
                [tr[s * 32 + eg * 4 : s * 32 + eg * 4 + 4, h * 64 : h * 64 + 48] for eg in range(8)], axis=1
            )
    rs[...] = rs32[...].astype(BF)
    pl.semaphore_wait(sem, COLS + ROWS - 2)

    own = at(col * 16, 16, 16)
    chip, core = lax.div(col, 2), lax.rem(col, 2)
    pltpu.make_async_copy(rs, rt.at[row], r1_recv).start()

    def send_right(s, _):
        pltpu.make_async_remote_copy(
            src_ref=rs, dst_ref=rt.at[row], send_sem=r1_send, recv_sem=r1_recv,
            device_id=(lax.rem(row + s, ROWS), col), device_id_type=MESH,
        ).start()
        return 0

    lax.fori_loop(1, ROWS, send_right, 0)

    for s in range(4):
        for g in range(22):
            qt, q = g // 4, g % 4
            a_ref[qt * 16 + s * 4 : qt * 16 + s * 4 + 4, q * 256 : q * 256 + 256] = mn[
                s, group_rows(g) : group_rows(g) + 4
            ]
    a_ref[80:96, 512:1024] = jnp.zeros((16, 512), F32)
    lm = jnp.concatenate(
        [
            lax.dot_general(a_ref[:, q * 256 : q * 256 + 256].astype(BF), f1[...], NT, preferred_element_type=F32)
            for q in range(4)
        ],
        axis=1,
    )
    for qt in range(6):
        ls[:, qt * 128 : qt * 128 + 128] = lm[qt * 16 : qt * 16 + 16].astype(BF)
    pltpu.make_async_copy(ls, lmsg.at[chip, core], l_recv).start()

    def send_left(s, _):
        pltpu.make_async_remote_copy(
            src_ref=ls, dst_ref=lmsg.at[chip, core], send_sem=l_send, recv_sem=l_recv,
            device_id=(row, lax.rem(col + 2 * s, COLS)), device_id_type=MESH,
        ).start()
        return 0

    lax.fori_loop(1, 8, send_left, 0)

    pltpu.make_async_copy(rt, rt, r1_recv).wait()
    own_half = pltpu.make_async_copy(rt.at[col // 2, col % 2], rmsg.at[own], r2_recv)
    own_half.start()

    def forward_right(s, _):
        t = lax.rem(col + s, COLS)
        pltpu.make_async_remote_copy(
            src_ref=rt.at[lax.div(t, 2), lax.rem(t, 2)], dst_ref=rmsg.at[own], send_sem=r2_send, recv_sem=r2_recv,
            device_id=(row, t), device_id_type=MESH,
        ).start()
        return 0

    lax.fori_loop(1, COLS, forward_right, 0)
    pltpu.make_async_copy(lmsg.at[:, core], lmsg.at[:, core], l_recv).wait()
    share = pltpu.make_async_remote_copy(
        src_ref=lmsg.at[:, core], dst_ref=lmsg.at[:, core], send_sem=l2_send, recv_sem=l2_recv,
        device_id=(row, col + 1 - 2 * core), device_id_type=MESH,
    )
    share.start()
    for load in loads[3:]:
        load.wait()
    wof[...] = wo[...].astype(F32)
    bd[...] = jnp.zeros(bd.shape, BF)

    def place(b, _):
        w = wof[pl.ds((b % 8) * 4 + b // 8, 32, stride=32), :].astype(BF)
        for q in range(4):
            bd[at(b * 128 + q * 32, 32, 32), q * 128 : q * 128 + 128] = w
        return 0

    lax.fori_loop(0, 32, place, 0, unroll=4)
    psf[...] = ps[...].reshape(CJ * RI, 128).astype(F32)
    wedge[0:256] = wl[...].T
    wedge[256:512] = wr[...].T
    pltpu.make_async_copy(rmsg, rmsg, r2_recv).wait()
    rmt[...] = rmsg[...].T

    def pick(u, _):
        a, b = iota((256, 256), 0), iota((256, 256), 1)
        for w in range(4):
            hit = ones_where((a // 4 == b // 4) & (a % 4 == w) & (b % 4 == u))
            rsel[u, w * 384 : w * 384 + 384] = jnp.dot(rmt[...], hit, preferred_element_type=F32).astype(BF)
        return 0

    lax.fori_loop(0, 4, pick, 0, unroll=4)
    share.wait()


    def cells_of(m):
        return lh.at[PARTS[m][2] : PARTS[m][3], at((chip * 8 + row) * 16, 16, 16), at(core * 128, 128, 128)]

    def scatter(m, o):
        z_row = [lax.rem(row + o + d, 4) for d in range(4)]
        k = lax.rem(col + lax.div(o, 4), 2)
        for b in range(4):
            for a in range(4):
                r = y_row[(a + b) % 4] + z_row[a]
                c = x_col[a] + y_col[(a + b) % 4] + k

                def start(r=r, c=c):
                    pltpu.make_async_remote_copy(
                        src_ref=send.at[r * COLS + c, PARTS[m][2] : PARTS[m][3]], dst_ref=cells_of(m),
                        send_sem=e_send.at[m], recv_sem=e_recv.at[m], device_id=(r, c), device_id_type=MESH,
                    ).start()

                if a or b:
                    start()
                else:
                    pl.when(o > 0)(start)

    for m, (lo, hi, t_lo, t_hi) in enumerate(PARTS):

        def outer(u, _, m=m):
            if m:
                scatter(m - 1, u)
            for w in range(4):
                x = jnp.dot(
                    rsel[u, w * 384 : w * 384 + 384],
                    lmsg[:, :, :, m * 384 : m * 384 + 384].reshape(256, 384),
                    preferred_element_type=F32,
                ) * (1.0 / 64)
                for eg in range(8):
                    for qt in range(3):
                        lhs[at(u * 144 + qt * 48, 48, 16), w * 1024 + eg * 128 : w * 1024 + eg * 128 + 128] = x[
                            eg * 48 : eg * 48 + 48, qt * 128 : qt * 128 + 128
                        ].astype(BF)
            return 0

        lax.fori_loop(0, 4, outer, 0, unroll=2)

        def project(u, _):
            rows = at(u * 288, 288, 16)
            osc[rows, :] = jnp.dot(lhs[rows, :], bd[...], preferred_element_type=F32)
            return 0

        lax.fori_loop(0, 2, project, 0)

        def normalize(ia, _, m=m, lo=lo, hi=hi, t_lo=t_lo, t_hi=t_hi):
            if m:
                pl.when(lax.rem(ia, 2) == 0)(lambda: scatter(m - 1, 4 + lax.div(ia, 2)))
            h, a = lax.div(ia, 4), lax.rem(ia, 4)
            for ib in range(lo, hi):
                g, u = slot(a, ib, h)
                upd = osc[at(u * 144 + lax.div(g, 4) * 48, 48, 8), at(lax.rem(g, 4) * 128, 128, 128)][:44]
                cells = pl.ds(44 * h + in_half(a, ib), CJ, stride=RI)
                v = psf[cells, :] + upd
                psf[cells, :] = v
                c = v - jnp.mean(v, axis=-1, keepdims=True)
                n = c * lax.rsqrt(jnp.mean(c * c, axis=-1, keepdims=True) + 1e-05)
                pn[ia, 44 * ib : 44 * ib + 44] = n
            if hi == 11:
                pn[ia, 484:512] = jnp.zeros((28, 128), F32)
            p = pn[ia, t_lo * 128 : t_hi * 128].astype(BF)
            proj = lax.dot_general(wedge[...], p, NT, preferred_element_type=F32)
            left = sigmoid(proj[0:128]) * proj[128:256]
            right = sigmoid(proj[256:384]) * proj[384:512]
            rows = at(ia * PITCH, 128, 8)
            for t in range(t_hi - t_lo):
                el[t, rows, :] = left[:, t * 128 : t * 128 + 128]
                er[t, rows, :] = right[:, t * 128 : t * 128 + 128]
            return 0

        lax.fori_loop(0, 8, normalize, 0, unroll=4)

        def pack(c, _, t_lo=t_lo, t_hi=t_hi):
            for t in range(t_hi - t_lo):
                cells = pl.ds(c, 8, stride=PITCH)
                send[c, t_lo + t] = jnp.concatenate([el[t, cells, :], er[t, cells, :]], axis=0).astype(BF)
            return 0

        lax.fori_loop(0, N, pack, 0, unroll=8)
        pltpu.make_async_copy(send.at[me, t_lo:t_hi], cells_of(m), e_recv.at[m]).start()

    def scatter_all(o, _):
        scatter(1, o)
        return 0

    lax.fori_loop(0, 8, scatter_all, 0)

    for t in range(4):
        lo, hi = SPAN[t]
        for b in range(lo, hi):
            f, n = iota((256, 128), 0), iota((256, 128), 1)
            k = n % 64
            hit = (f // 128 == n // 64) & (f % 128 + 128 * t == 44 * b + k) & (k < 44)
            sw[t, :, (b - lo) * 128 : (b - lo) * 128 + 128] = ones_where(hit)
            n, f = iota((128, 256), 0), iota((128, 256), 1)
            k = n % 16
            a = n % 64 // 16
            j = jnp.where(k < 6, 6 * a + k, 18 + 5 * a + k)
            hit = (f // 128 == n // 64) & (f % 128 + 128 * t == 44 * b + j) & (k < 11)
            s2[t, (b - lo) * 128 : (b - lo) * 128 + 128, :] = ones_where(hit)
    rop32[...] = jnp.zeros(rop32.shape, F32)

    def gates(ia, _):
        gate[ia] = sigmoid(jnp.dot(pn[ia].astype(BF), wg[...], preferred_element_type=F32))
        return 0

    lax.fori_loop(0, 8, gates, 0)

    for m, (_, _, t_lo, t_hi) in enumerate(PARTS):
        part = lh.at[t_lo:t_hi]
        pltpu.make_async_copy(part, part, e_recv.at[m]).wait()

        def widen(g, _, m=m):
            lo, hi = ((0, 5), (5, 11))[m]
            xs = {}
            for t in ((0, 1), (1, 2, 3))[m]:
                first, last = max(SPAN[t][0], lo), min(SPAN[t][1], hi)
                lanes = slice((first - SPAN[t][0]) * 128, (last - SPAN[t][0]) * 128)
                y = jnp.dot(lh[t, at(g * 256, 256, 256), :], sw[t, :, lanes], preferred_element_type=F32)
                for b in range(first, last):
                    x = y[:, (b - first) * 128 : (b - first) * 128 + 128]
                    xs[b] = xs[b] + x if b in xs else x
            for b, x in xs.items():
                x = x.reshape(2, 8, 2, 8, 128)
                for q in range(2):
                    p = 2 * g + q
                    lop[b * 64 : b * 64 + 64, at(p * 128, 128, 128)] = x[q, :, 0].reshape(64, 128).astype(BF)
                    for r in range(8):
                        rop32[p, pl.ds(r * 128 + b, 8, stride=16), :] = x[q, r, 1]
            return 0

        lax.fori_loop(0, 4, widen, 0, unroll=2)
    for p in range(8):
        rop[:, p * 128 : p * 128 + 128] = rop32[p].astype(BF)

    y0 = col // 2 % 2

    def product(step, _):
        odd, flip = step % 2, step // 2
        pairs = (
            2 * lax.rem(x + 2 - odd, 4) + (y0 + flip) % 2,
            2 * lax.rem(x + 3 * odd, 4) + (y0 + 1 + flip) % 2,
        )
        keys = jnp.concatenate([rop[at(p * 128, 128, 128), :] for p in pairs], axis=0)
        c = lax.dot_general(lop[...], keys, NT, preferred_element_type=F32).astype(BF)
        for q in range(2):
            for b in range(11):
                lhs2[q * 64 : q * 64 + 64, b * 128 : b * 128 + 128] = c[b * 64 : b * 64 + 64, q * 128 : q * 128 + 128]
        zs = []
        for t in range(4):
            lo, hi = SPAN[t]
            z = jnp.dot(lhs2[:, lo * 128 : hi * 128], s2[t, : (hi - lo) * 128, :], preferred_element_type=F32)
            zs.append(z.reshape(16, 8, 256))
        for h in range(2):
            z = jnp.concatenate([zs[2 * h], zs[2 * h + 1]], axis=1).astype(BF)
            for q in range(2):
                sb[h, at(pairs[q] * 8, 8, 8)] = z[8 * q : 8 * q + 8]

        for dr in range(ROWS):
            r = lax.rem(row + dr, ROWS)
            for k in range(2):
                for p in pairs:

                    def start(r=r, k=k, p=p):
                        pltpu.make_async_remote_copy(
                            src_ref=sb.at[:, p * 8 + r, :, k * 128 : k * 128 + 128], dst_ref=rv.at[me],
                            send_sem=c_send, recv_sem=c_recv.at[step], device_id=(r, 2 * p + k), device_id_type=MESH,
                        ).start()

                    if dr:
                        start()
                    else:
                        pl.when(2 * p + k != col)(start)
        return 0

    lax.fori_loop(0, 4, product, 0)
    back = sb.at[:, col // 2 * 8 + row, :, at(col % 2 * 128, 128, 128)]
    pltpu.make_async_copy(back, rv.at[me], c_recv.at[2]).start()

    for step in range(4):
        odd, flip = step % 2, step // 2
        part = rv.at[0 : N // 4]
        pltpu.make_async_copy(part, part, c_recv.at[step]).wait()
        for dx, dy in ((2 - odd, flip), (3 * odd, 1 + flip)):
            p = 2 * lax.rem(x + 4 - dx, 4) + lax.rem(y0 + dy, 2)

            def unpack(r, _, p=p):
                for k in range(2):
                    c = r * COLS + 2 * p + k
                    for h in range(2):
                        rc[h, at(c * PITCH2, 16, 8), :] = rv[c, h].astype(F32)
                return 0

            lax.fori_loop(0, ROWS, unpack, 0, unroll=4)

    def finish(ia, _):
        for t in range(4):
            z = rc[t // 2, pl.ds(t % 2 * 8 + ia, 128, stride=PITCH2), :]
            c = z - jnp.mean(z, axis=0, keepdims=True)
            n = (c * lax.rsqrt(jnp.mean(c * c, axis=0, keepdims=True) + 1e-05)).astype(BF)
            branch = lax.dot_general(n, wout[...], TN, preferred_element_type=F32)
            br[t * 128 : t * 128 + 128] = branch * gate[ia, t * 128 : t * 128 + 128]
        for ib in range(11):
            cells = pl.ds(44 * lax.div(ia, 4) + in_half(lax.rem(ia, 4), ib), CJ, stride=RI)
            psf[cells, :] = psf[cells, :] + br[44 * ib : 44 * ib + 44]
        return 0

    lax.fori_loop(0, 8, finish, 0, unroll=4)
    out[...] = psf[...].astype(BF).reshape(CJ, RI, 128)

    def sent(src, sem):
        pltpu.make_async_remote_copy(
            src_ref=src, dst_ref=src, send_sem=sem, recv_sem=l_recv, device_id=dev((me + 1) % N), device_id_type=MESH
        ).wait_send()

    sent(lmsg.at[0:7, 0], l_send)
    sent(rt.at[0:7], r1_send)
    sent(rmsg.at[0:240], r2_send)
    for m, (_, _, t_lo, t_hi) in enumerate(PARTS):
        sent(send.at[0 : N - 1, t_lo:t_hi], e_send.at[m])
    sent(rv.at[0 : N - 1], c_send)


def per_device(hf, ps, f1, f2, wo, wl, wr, wg, wout):
    dma = pltpu.SemaphoreType.DMA
    vm = pltpu.VMEM
    out = pl.pallas_call(
        kernel,
        out_shape=jax.ShapeDtypeStruct((CJ, RI, 128), BF),
        in_specs=[pl.BlockSpec(memory_space=pl.ANY)] * 9,
        out_specs=VM,
        scratch_shapes=[
            vm(hf.shape, BF), vm((CJ, RI, 128), BF), vm((32, 256), BF), vm((32, 256), BF), vm(wo.shape, BF),
            vm(wl.shape, BF), vm(wr.shape, BF), vm(wg.shape, BF), vm(wout.shape, BF),
            vm((96, 1024), F32), vm((128, 128), F32), vm((16, 768), BF), vm((2, 16, 384), F32), vm((2, 16, 384), BF),
            vm((8, 2, 16, 768), BF), vm((8, 2, 16, 384), BF), vm((256, 384), BF), vm((384, 256), BF), vm((1024, 128), F32),
            vm((4096, 512), BF), vm((576, 4096), BF), vm((576, 512), F32), vm((4, 1536, 256), BF), vm((CJ * RI, 128), F32),
            vm((8, 512, 128), F32), vm((2, 8 * PITCH, 128), F32), vm((2, 8 * PITCH, 128), F32), vm((512, 128), BF),
            vm((8, 512, 128), F32), vm((N, 4, 16, 128), BF), vm((4, 1024, 256), BF), vm((4, 256, 512), BF),
            vm((4, 512, 256), BF), vm((704, 1024), BF), vm((8, 1024, 128), F32), vm((1024, 1024), BF),
            vm((128, 1408), BF), vm((2, 64, 16, 256), BF), vm((N, 2, 16, 128), BF), vm((2, N * PITCH2, 128), F32),
            vm((512, 128), F32), dma((9,)), dma, dma, dma, dma, dma, dma, dma, dma, dma((2,)), dma((2,)), dma, dma((4,)),
        ],
        compiler_params=pltpu.CompilerParams(
            vmem_limit_bytes=60 * 2**20, collective_id=0, has_side_effects=True
        ),
    )(hf, ps.transpose(1, 0, 2), f1.T, f2.T, wo, wl, wr, wg, wout)
    return out.transpose(1, 0, 2)


def solution(mesh):
    return jax.shard_map(
        per_device,
        mesh=mesh,
        in_specs=(P("col", "row", None), P("row", "col", None), P(), P(), P(), P(), P(), P(), P()),
        out_specs=P("row", "col", None),
        check_vma=False,
    )
```

```python
import jax
import jax.numpy as jnp
from jax import lax
from jax.experimental import pallas as pl
from jax.experimental.pallas import tpu as pltpu
from jax.sharding import PartitionSpec as P

ROWS, COLS = 8, 16
N = ROWS * COLS
RI, CJ = 88, 44
PITCH, PITCH2 = 136, 24
MESH = pl.DeviceIdType.MESH
VM = pl.BlockSpec(memory_space=pltpu.VMEM)
F32, BF = jnp.float32, jnp.bfloat16
NT = (((1,), (1,)), ((), ()))
TN = (((0,), (0,)), ((), ()))
PARTS = ((0, 6, 0, 2), (6, 11, 2, 4))
SPAN = ((0, 3), (2, 6), (5, 9), (8, 11))


def in_half(a, b):
    return 6 * a + b if b < 6 else 24 + 5 * a + b - 6


def slot(a, b, h):
    i = in_half(a, b) - (0 if b < 6 else 24)
    return lax.div(i, 4) + h * (6 if b < 6 else 5), lax.rem(i, 4)


def group_rows(g):
    return 4 * (g if g < 6 else g + 5 if g < 12 else g - 6 if g < 17 else g)


def dev(flat):
    return (flat // COLS, flat % COLS)


def sigmoid(v):
    return 0.5 * jnp.tanh(0.5 * v) + 0.5


def iota(shape, dim):
    return lax.broadcasted_iota(jnp.int32, shape, dim)


def ones_where(mask):
    return mask.astype(F32).astype(BF)


def at(start, size, align):
    return pl.ds(pl.multiple_of(start, align), size)


def kernel(
    hf_any, ps_any, f1_any, f2_any, wo_any, wl_any, wr_any, wg_any, wout_any, out,
    hf, ps, f1, f2, wo, wl, wr, wg, wout,
    a_ref, p_ref, ls, rs32, rs, lmsg, rt, rmsg, rmt, wof, bd, lhs, osc, rsel, psf, pn, el, er, wedge, gate,
    send, lh, sw, s2, lop, rop32, rop, lhs2, sb, rv, rc, br,
    loaded, l2_send, l2_recv, l_send, l_recv, r1_send, r1_recv, r2_send, r2_recv, e_send, e_recv, c_send, c_recv,
):
    row, col = lax.axis_index("row"), lax.axis_index("col")
    me = row * COLS + col
    around = [lax.rem(col + c, COLS) for c in range(COLS)]
    x, y = col // 4, row // 4 * 2 + col // 2 % 2
    x_col = [lax.rem(x + d, 4) * 4 for d in range(4)]
    y_col = [lax.rem(lax.rem(y + d, 4), 2) * 2 for d in range(4)]
    y_row = [lax.div(lax.rem(y + d, 4), 2) * 4 for d in range(4)]
    sem = pltpu.get_barrier_semaphore()

    loads = [
        pltpu.make_async_copy(src, dst, loaded.at[n])
        for n, (src, dst) in enumerate(
            (
                (hf_any, hf), (f2_any, f2), (f1_any, f1), (wo_any, wo), (ps_any, ps), (wl_any, wl), (wr_any, wr),
                (wg_any, wg), (wout_any, wout),
            )
        )
    ]
    for load in loads:
        load.start()

    for c in range(1, COLS):
        pl.semaphore_signal(sem, inc=1, device_id=(row, around[c]), device_id_type=MESH)
    for r in range(1, ROWS):
        pl.semaphore_signal(sem, inc=1, device_id=(lax.rem(row + r, ROWS), col), device_id_type=MESH)

    for load in loads[:3]:
        load.wait()
    v = hf[...].astype(F32)
    centered = v - jnp.mean(v, axis=-1, keepdims=True)
    mn = centered * lax.rsqrt(jnp.mean(centered * centered, axis=-1, keepdims=True) + 1e-05)
    pr = jnp.concatenate(
        [lax.dot_general(mn[s].astype(BF), f2[...], NT, preferred_element_type=F32) for s in range(4)], axis=1
    )
    p_ref[...] = jnp.zeros(p_ref.shape, F32)
    p_ref[0:44] = pr[0:44]
    p_ref[64:108] = pr[44:88]
    tr = p_ref[...].T
    for h in range(2):
        for s in range(4):
            rs32[h, s * 4 : s * 4 + 4, :] = jnp.concatenate(
                [tr[s * 32 + eg * 4 : s * 32 + eg * 4 + 4, h * 64 : h * 64 + 48] for eg in range(8)], axis=1
            )
    rs[...] = rs32[...].astype(BF)
    pl.semaphore_wait(sem, COLS + ROWS - 2)

    own = at(col * 16, 16, 16)
    chip, core = lax.div(col, 2), lax.rem(col, 2)
    pltpu.make_async_copy(rs, rt.at[row], r1_recv).start()

    def send_right(s, _):
        pltpu.make_async_remote_copy(
            src_ref=rs, dst_ref=rt.at[row], send_sem=r1_send, recv_sem=r1_recv,
            device_id=(lax.rem(row + s, ROWS), col), device_id_type=MESH,
        ).start()
        return 0

    lax.fori_loop(1, ROWS, send_right, 0)

    for s in range(4):
        for g in range(22):
            qt, q = g // 4, g % 4
            a_ref[qt * 16 + s * 4 : qt * 16 + s * 4 + 4, q * 256 : q * 256 + 256] = mn[
                s, group_rows(g) : group_rows(g) + 4
            ]
    a_ref[80:96, 512:1024] = jnp.zeros((16, 512), F32)
    lm = jnp.concatenate(
        [
            lax.dot_general(a_ref[:, q * 256 : q * 256 + 256].astype(BF), f1[...], NT, preferred_element_type=F32)
            for q in range(4)
        ],
        axis=1,
    )
    for qt in range(6):
        ls[:, qt * 128 : qt * 128 + 128] = lm[qt * 16 : qt * 16 + 16].astype(BF)
    pltpu.make_async_copy(ls, lmsg.at[chip, core], l_recv).start()

    def send_left(s, _):
        pltpu.make_async_remote_copy(
            src_ref=ls, dst_ref=lmsg.at[chip, core], send_sem=l_send, recv_sem=l_recv,
            device_id=(row, lax.rem(col + 2 * s, COLS)), device_id_type=MESH,
        ).start()
        return 0

    lax.fori_loop(1, 8, send_left, 0)

    pltpu.make_async_copy(rt, rt, r1_recv).wait()
    own_half = pltpu.make_async_copy(rt.at[col // 2, col % 2], rmsg.at[own], r2_recv)
    own_half.start()

    def forward_right(s, _):
        t = lax.rem(col + s, COLS)
        pltpu.make_async_remote_copy(
            src_ref=rt.at[lax.div(t, 2), lax.rem(t, 2)], dst_ref=rmsg.at[own], send_sem=r2_send, recv_sem=r2_recv,
            device_id=(row, t), device_id_type=MESH,
        ).start()
        return 0

    lax.fori_loop(1, COLS, forward_right, 0)
    pltpu.make_async_copy(lmsg.at[:, core], lmsg.at[:, core], l_recv).wait()
    share = pltpu.make_async_remote_copy(
        src_ref=lmsg.at[:, core], dst_ref=lmsg.at[:, core], send_sem=l2_send, recv_sem=l2_recv,
        device_id=(row, col + 1 - 2 * core), device_id_type=MESH,
    )
    share.start()
    for load in loads[3:]:
        load.wait()
    wof[...] = wo[...].astype(F32)
    bd[...] = jnp.zeros(bd.shape, BF)

    def place(b, _):
        w = wof[pl.ds((b % 8) * 4 + b // 8, 32, stride=32), :].astype(BF)
        for q in range(4):
            bd[at(b * 128 + q * 32, 32, 32), q * 128 : q * 128 + 128] = w
        return 0

    lax.fori_loop(0, 32, place, 0, unroll=4)
    psf[...] = ps[...].reshape(CJ * RI, 128).astype(F32)
    wedge[0:256] = wl[...].T
    wedge[256:512] = wr[...].T
    pltpu.make_async_copy(rmsg, rmsg, r2_recv).wait()
    rmt[...] = rmsg[...].T

    def pick(u, _):
        a, b = iota((256, 256), 0), iota((256, 256), 1)
        for w in range(4):
            hit = ones_where((a // 4 == b // 4) & (a % 4 == w) & (b % 4 == u))
            rsel[u, w * 384 : w * 384 + 384] = jnp.dot(rmt[...], hit, preferred_element_type=F32).astype(BF)
        return 0

    lax.fori_loop(0, 4, pick, 0, unroll=4)
    share.wait()


    def cells_of(m):
        return lh.at[PARTS[m][2] : PARTS[m][3], at((chip * 8 + row) * 16, 16, 16), at(core * 128, 128, 128)]

    def scatter(m, o):
        z_row = [lax.rem(row + o + d, 4) for d in range(4)]
        k = lax.rem(col + lax.div(o, 4), 2)
        for b in range(4):
            for a in range(4):
                r = y_row[(a + b) % 4] + z_row[a]
                c = x_col[a] + y_col[(a + b) % 4] + k

                def start(r=r, c=c):
                    pltpu.make_async_remote_copy(
                        src_ref=send.at[r * COLS + c, PARTS[m][2] : PARTS[m][3]], dst_ref=cells_of(m),
                        send_sem=e_send.at[m], recv_sem=e_recv.at[m], device_id=(r, c), device_id_type=MESH,
                    ).start()

                if a or b:
                    start()
                else:
                    pl.when(o > 0)(start)

    for m, (lo, hi, t_lo, t_hi) in enumerate(PARTS):

        def outer(u, _, m=m):
            if m:
                scatter(m - 1, u)
            for w in range(4):
                x = jnp.dot(
                    rsel[u, w * 384 : w * 384 + 384],
                    lmsg[:, :, :, m * 384 : m * 384 + 384].reshape(256, 384),
                    preferred_element_type=F32,
                ) * (1.0 / 64)
                for eg in range(8):
                    for qt in range(3):
                        lhs[at(u * 144 + qt * 48, 48, 16), w * 1024 + eg * 128 : w * 1024 + eg * 128 + 128] = x[
                            eg * 48 : eg * 48 + 48, qt * 128 : qt * 128 + 128
                        ].astype(BF)
            return 0

        lax.fori_loop(0, 4, outer, 0, unroll=4)

        def project(u, _):
            rows = at(u * 288, 288, 16)
            osc[rows, :] = jnp.dot(lhs[rows, :], bd[...], preferred_element_type=F32)
            return 0

        lax.fori_loop(0, 2, project, 0, unroll=2)

        def normalize(ia, _, m=m, lo=lo, hi=hi, t_lo=t_lo, t_hi=t_hi):
            if m:
                pl.when(lax.rem(ia, 2) == 0)(lambda: scatter(m - 1, 4 + lax.div(ia, 2)))
            h, a = lax.div(ia, 4), lax.rem(ia, 4)
            for ib in range(lo, hi):
                g, u = slot(a, ib, h)
                upd = osc[at(u * 144 + lax.div(g, 4) * 48, 48, 8), at(lax.rem(g, 4) * 128, 128, 128)][:44]
                cells = pl.ds(44 * h + in_half(a, ib), CJ, stride=RI)
                v = psf[cells, :] + upd
                psf[cells, :] = v
                c = v - jnp.mean(v, axis=-1, keepdims=True)
                n = c * lax.rsqrt(jnp.mean(c * c, axis=-1, keepdims=True) + 1e-05)
                pn[ia, 44 * ib : 44 * ib + 44] = n
            if hi == 11:
                pn[ia, 484:512] = jnp.zeros((28, 128), F32)
            p = pn[ia, t_lo * 128 : t_hi * 128].astype(BF)
            proj = lax.dot_general(wedge[...], p, NT, preferred_element_type=F32)
            left = sigmoid(proj[0:128]) * proj[128:256]
            right = sigmoid(proj[256:384]) * proj[384:512]
            rows = at(ia * PITCH, 128, 8)
            for t in range(t_hi - t_lo):
                el[t, rows, :] = left[:, t * 128 : t * 128 + 128]
                er[t, rows, :] = right[:, t * 128 : t * 128 + 128]
            return 0

        lax.fori_loop(0, 8, normalize, 0, unroll=8)

        def pack(c, _, t_lo=t_lo, t_hi=t_hi):
            for t in range(t_hi - t_lo):
                cells = pl.ds(c, 8, stride=PITCH)
                send[c, t_lo + t] = jnp.concatenate([el[t, cells, :], er[t, cells, :]], axis=0).astype(BF)
            return 0

        lax.fori_loop(0, N, pack, 0, unroll=16)
        pltpu.make_async_copy(send.at[me, t_lo:t_hi], cells_of(m), e_recv.at[m]).start()

    def scatter_all(o, _):
        scatter(1, o)
        return 0

    lax.fori_loop(0, 8, scatter_all, 0)

    for t in range(4):
        lo, hi = SPAN[t]
        for b in range(lo, hi):
            f, n = iota((256, 128), 0), iota((256, 128), 1)
            k = n % 64
            hit = (f // 128 == n // 64) & (f % 128 + 128 * t == 44 * b + k) & (k < 44)
            sw[t, :, (b - lo) * 128 : (b - lo) * 128 + 128] = ones_where(hit)
            n, f = iota((128, 256), 0), iota((128, 256), 1)
            k = n % 16
            a = n % 64 // 16
            j = jnp.where(k < 6, 6 * a + k, 18 + 5 * a + k)
            hit = (f // 128 == n // 64) & (f % 128 + 128 * t == 44 * b + j) & (k < 11)
            s2[t, (b - lo) * 128 : (b - lo) * 128 + 128, :] = ones_where(hit)
    rop32[...] = jnp.zeros(rop32.shape, F32)

    def gates(ia, _):
        gate[ia] = sigmoid(jnp.dot(pn[ia].astype(BF), wg[...], preferred_element_type=F32))
        return 0

    lax.fori_loop(0, 8, gates, 0)

    for m, (_, _, t_lo, t_hi) in enumerate(PARTS):
        part = lh.at[t_lo:t_hi]
        pltpu.make_async_copy(part, part, e_recv.at[m]).wait()

        def widen(g, _, m=m):
            lo, hi = ((0, 5), (5, 11))[m]
            xs = {}
            for t in ((0, 1), (1, 2, 3))[m]:
                first, last = max(SPAN[t][0], lo), min(SPAN[t][1], hi)
                lanes = slice((first - SPAN[t][0]) * 128, (last - SPAN[t][0]) * 128)
                y = jnp.dot(lh[t, at(g * 256, 256, 256), :], sw[t, :, lanes], preferred_element_type=F32)
                for b in range(first, last):
                    x = y[:, (b - first) * 128 : (b - first) * 128 + 128]
                    xs[b] = xs[b] + x if b in xs else x
            for b, x in xs.items():
                x = x.reshape(2, 8, 2, 8, 128)
                for q in range(2):
                    p = 2 * g + q
                    lop[b * 64 : b * 64 + 64, at(p * 128, 128, 128)] = x[q, :, 0].reshape(64, 128).astype(BF)
                    for r in range(8):
                        rop32[p, pl.ds(r * 128 + b, 8, stride=16), :] = x[q, r, 1]
            return 0

        lax.fori_loop(0, 4, widen, 0, unroll=2)
    for p in range(8):
        rop[:, p * 128 : p * 128 + 128] = rop32[p].astype(BF)

    y0 = col // 2 % 2

    def product(step, _):
        odd, flip = step % 2, step // 2
        pairs = (
            2 * lax.rem(x + 2 - odd, 4) + (y0 + flip) % 2,
            2 * lax.rem(x + 3 * odd, 4) + (y0 + 1 + flip) % 2,
        )
        keys = jnp.concatenate([rop[at(p * 128, 128, 128), :] for p in pairs], axis=0)
        c = lax.dot_general(lop[...], keys, NT, preferred_element_type=F32).astype(BF)
        for q in range(2):
            for b in range(11):
                lhs2[q * 64 : q * 64 + 64, b * 128 : b * 128 + 128] = c[b * 64 : b * 64 + 64, q * 128 : q * 128 + 128]
        zs = []
        for t in range(4):
            lo, hi = SPAN[t]
            z = jnp.dot(lhs2[:, lo * 128 : hi * 128], s2[t, : (hi - lo) * 128, :], preferred_element_type=F32)
            zs.append(z.reshape(16, 8, 256))
        for h in range(2):
            z = jnp.concatenate([zs[2 * h], zs[2 * h + 1]], axis=1).astype(BF)
            for q in range(2):
                sb[h, at(pairs[q] * 8, 8, 8)] = z[8 * q : 8 * q + 8]

        for dr in range(ROWS):
            r = lax.rem(row + dr, ROWS)
            for k in range(2):
                for p in pairs:

                    def start(r=r, k=k, p=p):
                        pltpu.make_async_remote_copy(
                            src_ref=sb.at[:, p * 8 + r, :, k * 128 : k * 128 + 128], dst_ref=rv.at[me],
                            send_sem=c_send, recv_sem=c_recv.at[step], device_id=(r, 2 * p + k), device_id_type=MESH,
                        ).start()

                    if dr:
                        start()
                    else:
                        pl.when(2 * p + k != col)(start)
        return 0

    lax.fori_loop(0, 4, product, 0)
    back = sb.at[:, col // 2 * 8 + row, :, at(col % 2 * 128, 128, 128)]
    pltpu.make_async_copy(back, rv.at[me], c_recv.at[2]).start()

    for step in range(4):
        odd, flip = step % 2, step // 2
        part = rv.at[0 : N // 4]
        pltpu.make_async_copy(part, part, c_recv.at[step]).wait()
        for dx, dy in ((2 - odd, flip), (3 * odd, 1 + flip)):
            p = 2 * lax.rem(x + 4 - dx, 4) + lax.rem(y0 + dy, 2)

            def unpack(r, _, p=p):
                for k in range(2):
                    c = r * COLS + 2 * p + k
                    for h in range(2):
                        rc[h, at(c * PITCH2, 16, 8), :] = rv[c, h].astype(F32)
                return 0

            lax.fori_loop(0, ROWS, unpack, 0, unroll=4)

    def finish(ia, _):
        for t in range(4):
            z = rc[t // 2, pl.ds(t % 2 * 8 + ia, 128, stride=PITCH2), :]
            c = z - jnp.mean(z, axis=0, keepdims=True)
            n = (c * lax.rsqrt(jnp.mean(c * c, axis=0, keepdims=True) + 1e-05)).astype(BF)
            branch = lax.dot_general(n, wout[...], TN, preferred_element_type=F32)
            br[t * 128 : t * 128 + 128] = branch * gate[ia, t * 128 : t * 128 + 128]
        for ib in range(11):
            cells = pl.ds(44 * lax.div(ia, 4) + in_half(lax.rem(ia, 4), ib), CJ, stride=RI)
            psf[cells, :] = psf[cells, :] + br[44 * ib : 44 * ib + 44]
        return 0

    lax.fori_loop(0, 8, finish, 0, unroll=8)
    out[...] = psf[...].astype(BF).reshape(CJ, RI, 128)

    def sent(src, sem):
        pltpu.make_async_remote_copy(
            src_ref=src, dst_ref=src, send_sem=sem, recv_sem=l_recv, device_id=dev((me + 1) % N), device_id_type=MESH
        ).wait_send()

    sent(lmsg.at[0:7, 0], l_send)
    sent(rt.at[0:7], r1_send)
    sent(rmsg.at[0:240], r2_send)
    for m, (_, _, t_lo, t_hi) in enumerate(PARTS):
        sent(send.at[0 : N - 1, t_lo:t_hi], e_send.at[m])
    sent(rv.at[0 : N - 1], c_send)


def per_device(hf, ps, f1, f2, wo, wl, wr, wg, wout):
    dma = pltpu.SemaphoreType.DMA
    vm = pltpu.VMEM
    out = pl.pallas_call(
        kernel,
        out_shape=jax.ShapeDtypeStruct((CJ, RI, 128), BF),
        in_specs=[pl.BlockSpec(memory_space=pl.ANY)] * 9,
        out_specs=VM,
        scratch_shapes=[
            vm(hf.shape, BF), vm((CJ, RI, 128), BF), vm((32, 256), BF), vm((32, 256), BF), vm(wo.shape, BF),
            vm(wl.shape, BF), vm(wr.shape, BF), vm(wg.shape, BF), vm(wout.shape, BF),
            vm((96, 1024), F32), vm((128, 128), F32), vm((16, 768), BF), vm((2, 16, 384), F32), vm((2, 16, 384), BF),
            vm((8, 2, 16, 768), BF), vm((8, 2, 16, 384), BF), vm((256, 384), BF), vm((384, 256), BF), vm((1024, 128), F32),
            vm((4096, 512), BF), vm((576, 4096), BF), vm((576, 512), F32), vm((4, 1536, 256), BF), vm((CJ * RI, 128), F32),
            vm((8, 512, 128), F32), vm((2, 8 * PITCH, 128), F32), vm((2, 8 * PITCH, 128), F32), vm((512, 128), BF),
            vm((8, 512, 128), F32), vm((N, 4, 16, 128), BF), vm((4, 1024, 256), BF), vm((4, 256, 512), BF),
            vm((4, 512, 256), BF), vm((704, 1024), BF), vm((8, 1024, 128), F32), vm((1024, 1024), BF),
            vm((128, 1408), BF), vm((2, 64, 16, 256), BF), vm((N, 2, 16, 128), BF), vm((2, N * PITCH2, 128), F32),
            vm((512, 128), F32), dma((9,)), dma, dma, dma, dma, dma, dma, dma, dma, dma((2,)), dma((2,)), dma, dma((4,)),
        ],
        compiler_params=pltpu.CompilerParams(
            vmem_limit_bytes=60 * 2**20, collective_id=0, has_side_effects=True
        ),
    )(hf, ps.transpose(1, 0, 2), f1.T, f2.T, wo, wl, wr, wg, wout)
    return out.transpose(1, 0, 2)


def solution(mesh):
    return jax.shard_map(
        per_device,
        mesh=mesh,
        in_specs=(P("col", "row", None), P("row", "col", None), P(), P(), P(), P(), P(), P(), P()),
        out_specs=P("row", "col", None),
        check_vma=False,
    )
```

```python
import jax
import jax.numpy as jnp
from jax import lax
from jax.experimental import pallas as pl
from jax.experimental.pallas import tpu as pltpu
from jax.sharding import PartitionSpec as P

ROWS, COLS = 8, 16
N = ROWS * COLS
RI, CJ = 88, 44
PITCH, PITCH2 = 136, 24
MESH = pl.DeviceIdType.MESH
VM = pl.BlockSpec(memory_space=pltpu.VMEM)
F32, BF = jnp.float32, jnp.bfloat16
NT = (((1,), (1,)), ((), ()))
TN = (((0,), (0,)), ((), ()))
PARTS = ((0, 6, 0, 2), (6, 11, 2, 4))
SPAN = ((0, 3), (2, 6), (5, 9), (8, 11))


def in_half(a, b):
    return 6 * a + b if b < 6 else 24 + 5 * a + b - 6


def slot(a, b, h):
    i = in_half(a, b) - (0 if b < 6 else 24)
    return lax.div(i, 4) + h * (6 if b < 6 else 5), lax.rem(i, 4)


def group_rows(g):
    return 4 * (g if g < 6 else g + 5 if g < 12 else g - 6 if g < 17 else g)


def dev(flat):
    return (flat // COLS, flat % COLS)


def sigmoid(v):
    return 0.5 * jnp.tanh(0.5 * v) + 0.5


def iota(shape, dim):
    return lax.broadcasted_iota(jnp.int32, shape, dim)


def ones_where(mask):
    return mask.astype(F32).astype(BF)


def at(start, size, align):
    return pl.ds(pl.multiple_of(start, align), size)


def kernel(
    hf_any, ps_any, f1_any, f2_any, wo_any, wl_any, wr_any, wg_any, wout_any, out,
    hf, ps, f1, f2, wo, wl, wr, wg, wout,
    a_ref, p_ref, ls, rs32, rs, lmsg, rt, rmsg, rmt, wof, bd, lhs, osc, rsel, psf, pn, el, er, wedge, gate,
    send, lh, sw, s2, lop, rop32, rop, lhs2, sb, rv, rc, br,
    loaded, l2_send, l2_recv, l_send, l_recv, r1_send, r1_recv, r2_send, r2_recv, e_send, e_recv, c_send, c_recv,
):
    row, col = lax.axis_index("row"), lax.axis_index("col")
    me = row * COLS + col
    around = [lax.rem(col + c, COLS) for c in range(COLS)]
    x, y = col // 4, row // 4 * 2 + col // 2 % 2
    x_col = [lax.rem(x + d, 4) * 4 for d in range(4)]
    y_col = [lax.rem(lax.rem(y + d, 4), 2) * 2 for d in range(4)]
    y_row = [lax.div(lax.rem(y + d, 4), 2) * 4 for d in range(4)]
    sem = pltpu.get_barrier_semaphore()

    loads = [
        pltpu.make_async_copy(src, dst, loaded.at[n])
        for n, (src, dst) in enumerate(
            (
                (hf_any, hf), (f2_any, f2), (f1_any, f1), (wo_any, wo), (ps_any, ps), (wl_any, wl), (wr_any, wr),
                (wg_any, wg), (wout_any, wout),
            )
        )
    ]
    for load in loads:
        load.start()

    for c in range(1, COLS):
        pl.semaphore_signal(sem, inc=1, device_id=(row, around[c]), device_id_type=MESH)
    for r in range(1, ROWS):
        pl.semaphore_signal(sem, inc=1, device_id=(lax.rem(row + r, ROWS), col), device_id_type=MESH)

    for load in loads[:3]:
        load.wait()
    v = hf[...].astype(F32)
    centered = v - jnp.mean(v, axis=-1, keepdims=True)
    mn = centered * lax.rsqrt(jnp.mean(centered * centered, axis=-1, keepdims=True) + 1e-05)
    pr = jnp.concatenate(
        [lax.dot_general(mn[s].astype(BF), f2[...], NT, preferred_element_type=F32) for s in range(4)], axis=1
    )
    p_ref[...] = jnp.zeros(p_ref.shape, F32)
    p_ref[0:44] = pr[0:44]
    p_ref[64:108] = pr[44:88]
    tr = p_ref[...].T
    for h in range(2):
        for s in range(4):
            rs32[h, s * 4 : s * 4 + 4, :] = jnp.concatenate(
                [tr[s * 32 + eg * 4 : s * 32 + eg * 4 + 4, h * 64 : h * 64 + 48] for eg in range(8)], axis=1
            )
    rs[...] = rs32[...].astype(BF)
    pl.semaphore_wait(sem, COLS + ROWS - 2)

    own = at(col * 16, 16, 16)
    chip, core = lax.div(col, 2), lax.rem(col, 2)
    pltpu.make_async_copy(rs, rt.at[row], r1_recv).start()

    def send_right(s, _):
        pltpu.make_async_remote_copy(
            src_ref=rs, dst_ref=rt.at[row], send_sem=r1_send, recv_sem=r1_recv,
            device_id=(lax.rem(row + s, ROWS), col), device_id_type=MESH,
        ).start()
        return 0

    lax.fori_loop(1, ROWS, send_right, 0)

    for s in range(4):
        for g in range(22):
            qt, q = g // 4, g % 4
            a_ref[qt * 16 + s * 4 : qt * 16 + s * 4 + 4, q * 256 : q * 256 + 256] = mn[
                s, group_rows(g) : group_rows(g) + 4
            ]
    a_ref[80:96, 512:1024] = jnp.zeros((16, 512), F32)
    lm = jnp.concatenate(
        [
            lax.dot_general(a_ref[:, q * 256 : q * 256 + 256].astype(BF), f1[...], NT, preferred_element_type=F32)
            for q in range(4)
        ],
        axis=1,
    )
    for qt in range(6):
        ls[:, qt * 128 : qt * 128 + 128] = lm[qt * 16 : qt * 16 + 16].astype(BF)
    pltpu.make_async_copy(ls, lmsg.at[chip, core], l_recv).start()

    def send_left(s, _):
        pltpu.make_async_remote_copy(
            src_ref=ls, dst_ref=lmsg.at[chip, core], send_sem=l_send, recv_sem=l_recv,
            device_id=(row, lax.rem(col + 2 * s, COLS)), device_id_type=MESH,
        ).start()
        return 0

    lax.fori_loop(1, 8, send_left, 0)

    pltpu.make_async_copy(rt, rt, r1_recv).wait()
    own_half = pltpu.make_async_copy(rt.at[col // 2, col % 2], rmsg.at[own], r2_recv)
    own_half.start()

    def forward_right(s, _):
        t = lax.rem(col + s, COLS)
        pltpu.make_async_remote_copy(
            src_ref=rt.at[lax.div(t, 2), lax.rem(t, 2)], dst_ref=rmsg.at[own], send_sem=r2_send, recv_sem=r2_recv,
            device_id=(row, t), device_id_type=MESH,
        ).start()
        return 0

    lax.fori_loop(1, COLS, forward_right, 0)
    pltpu.make_async_copy(lmsg.at[:, core], lmsg.at[:, core], l_recv).wait()
    share = pltpu.make_async_remote_copy(
        src_ref=lmsg.at[:, core], dst_ref=lmsg.at[:, core], send_sem=l2_send, recv_sem=l2_recv,
        device_id=(row, col + 1 - 2 * core), device_id_type=MESH,
    )
    share.start()
    for load in loads[3:]:
        load.wait()
    wof[...] = wo[...].astype(F32)
    bd[...] = jnp.zeros(bd.shape, BF)

    def place(b, _):
        w = wof[pl.ds((b % 8) * 4 + b // 8, 32, stride=32), :].astype(BF)
        for q in range(4):
            bd[at(b * 128 + q * 32, 32, 32), q * 128 : q * 128 + 128] = w
        return 0

    lax.fori_loop(0, 32, place, 0, unroll=16)
    psf[...] = ps[...].reshape(CJ * RI, 128).astype(F32)
    wedge[0:256] = wl[...].T
    wedge[256:512] = wr[...].T
    pltpu.make_async_copy(rmsg, rmsg, r2_recv).wait()
    rmt[...] = rmsg[...].T

    def pick(u, _):
        a, b = iota((256, 256), 0), iota((256, 256), 1)
        for w in range(4):
            hit = ones_where((a // 4 == b // 4) & (a % 4 == w) & (b % 4 == u))
            rsel[u, w * 384 : w * 384 + 384] = jnp.dot(rmt[...], hit, preferred_element_type=F32).astype(BF)
        return 0

    lax.fori_loop(0, 4, pick, 0, unroll=4)
    share.wait()


    def cells_of(m):
        return lh.at[PARTS[m][2] : PARTS[m][3], at((chip * 8 + row) * 16, 16, 16), at(core * 128, 128, 128)]

    def scatter(m, o):
        z_row = [lax.rem(row + o + d, 4) for d in range(4)]
        k = lax.rem(col + lax.div(o, 4), 2)
        for b in range(4):
            for a in range(4):
                r = y_row[(a + b) % 4] + z_row[a]
                c = x_col[a] + y_col[(a + b) % 4] + k

                def start(r=r, c=c):
                    pltpu.make_async_remote_copy(
                        src_ref=send.at[r * COLS + c, PARTS[m][2] : PARTS[m][3]], dst_ref=cells_of(m),
                        send_sem=e_send.at[m], recv_sem=e_recv.at[m], device_id=(r, c), device_id_type=MESH,
                    ).start()

                if a or b:
                    start()
                else:
                    pl.when(o > 0)(start)

    for m, (lo, hi, t_lo, t_hi) in enumerate(PARTS):

        def outer(u, _, m=m):
            if m:
                scatter(m - 1, u)
            for w in range(4):
                x = jnp.dot(
                    rsel[u, w * 384 : w * 384 + 384],
                    lmsg[:, :, :, m * 384 : m * 384 + 384].reshape(256, 384),
                    preferred_element_type=F32,
                ) * (1.0 / 64)
                for eg in range(8):
                    for qt in range(3):
                        lhs[at(u * 144 + qt * 48, 48, 16), w * 1024 + eg * 128 : w * 1024 + eg * 128 + 128] = x[
                            eg * 48 : eg * 48 + 48, qt * 128 : qt * 128 + 128
                        ].astype(BF)
            return 0

        lax.fori_loop(0, 4, outer, 0, unroll=4)

        def project(u, _):
            rows = at(u * 288, 288, 16)
            osc[rows, :] = jnp.dot(lhs[rows, :], bd[...], preferred_element_type=F32)
            return 0

        lax.fori_loop(0, 2, project, 0, unroll=2)

        def normalize(ia, _, m=m, lo=lo, hi=hi, t_lo=t_lo, t_hi=t_hi):
            if m:
                pl.when(lax.rem(ia, 2) == 0)(lambda: scatter(m - 1, 4 + lax.div(ia, 2)))
            h, a = lax.div(ia, 4), lax.rem(ia, 4)
            for ib in range(lo, hi):
                g, u = slot(a, ib, h)
                upd = osc[at(u * 144 + lax.div(g, 4) * 48, 48, 8), at(lax.rem(g, 4) * 128, 128, 128)][:44]
                cells = pl.ds(44 * h + in_half(a, ib), CJ, stride=RI)
                v = psf[cells, :] + upd
                psf[cells, :] = v
                c = v - jnp.mean(v, axis=-1, keepdims=True)
                n = c * lax.rsqrt(jnp.mean(c * c, axis=-1, keepdims=True) + 1e-05)
                pn[ia, 44 * ib : 44 * ib + 44] = n
            if hi == 11:
                pn[ia, 484:512] = jnp.zeros((28, 128), F32)
            p = pn[ia, t_lo * 128 : t_hi * 128].astype(BF)
            proj = lax.dot_general(wedge[...], p, NT, preferred_element_type=F32)
            left = sigmoid(proj[0:128]) * proj[128:256]
            right = sigmoid(proj[256:384]) * proj[384:512]
            rows = at(ia * PITCH, 128, 8)
            for t in range(t_hi - t_lo):
                el[t, rows, :] = left[:, t * 128 : t * 128 + 128]
                er[t, rows, :] = right[:, t * 128 : t * 128 + 128]
            return 0

        lax.fori_loop(0, 8, normalize, 0, unroll=8)

        def pack(c, _, t_lo=t_lo, t_hi=t_hi):
            for t in range(t_hi - t_lo):
                cells = pl.ds(c, 8, stride=PITCH)
                send[c, t_lo + t] = jnp.concatenate([el[t, cells, :], er[t, cells, :]], axis=0).astype(BF)
            return 0

        lax.fori_loop(0, N, pack, 0, unroll=16)
        pltpu.make_async_copy(send.at[me, t_lo:t_hi], cells_of(m), e_recv.at[m]).start()

    def scatter_all(o, _):
        scatter(1, o)
        return 0

    lax.fori_loop(0, 8, scatter_all, 0)

    for t in range(4):
        lo, hi = SPAN[t]
        for b in range(lo, hi):
            f, n = iota((256, 128), 0), iota((256, 128), 1)
            k = n % 64
            hit = (f // 128 == n // 64) & (f % 128 + 128 * t == 44 * b + k) & (k < 44)
            sw[t, :, (b - lo) * 128 : (b - lo) * 128 + 128] = ones_where(hit)
            n, f = iota((128, 256), 0), iota((128, 256), 1)
            k = n % 16
            a = n % 64 // 16
            j = jnp.where(k < 6, 6 * a + k, 18 + 5 * a + k)
            hit = (f // 128 == n // 64) & (f % 128 + 128 * t == 44 * b + j) & (k < 11)
            s2[t, (b - lo) * 128 : (b - lo) * 128 + 128, :] = ones_where(hit)
    rop32[...] = jnp.zeros(rop32.shape, F32)

    def gates(ia, _):
        gate[ia] = sigmoid(jnp.dot(pn[ia].astype(BF), wg[...], preferred_element_type=F32))
        return 0

    lax.fori_loop(0, 8, gates, 0)

    for m, (_, _, t_lo, t_hi) in enumerate(PARTS):
        part = lh.at[t_lo:t_hi]
        pltpu.make_async_copy(part, part, e_recv.at[m]).wait()

        def widen(g, _, m=m):
            lo, hi = ((0, 5), (5, 11))[m]
            xs = {}
            for t in ((0, 1), (1, 2, 3))[m]:
                first, last = max(SPAN[t][0], lo), min(SPAN[t][1], hi)
                lanes = slice((first - SPAN[t][0]) * 128, (last - SPAN[t][0]) * 128)
                y = jnp.dot(lh[t, at(g * 256, 256, 256), :], sw[t, :, lanes], preferred_element_type=F32)
                for b in range(first, last):
                    x = y[:, (b - first) * 128 : (b - first) * 128 + 128]
                    xs[b] = xs[b] + x if b in xs else x
            for b, x in xs.items():
                x = x.reshape(2, 8, 2, 8, 128)
                for q in range(2):
                    p = 2 * g + q
                    lop[b * 64 : b * 64 + 64, at(p * 128, 128, 128)] = x[q, :, 0].reshape(64, 128).astype(BF)
                    for r in range(8):
                        rop32[p, pl.ds(r * 128 + b, 8, stride=16), :] = x[q, r, 1]
            return 0

        lax.fori_loop(0, 4, widen, 0, unroll=4)
    for p in range(8):
        rop[:, p * 128 : p * 128 + 128] = rop32[p].astype(BF)

    y0 = col // 2 % 2

    def product(step, _):
        odd, flip = step % 2, step // 2
        pairs = (
            2 * lax.rem(x + 2 - odd, 4) + (y0 + flip) % 2,
            2 * lax.rem(x + 3 * odd, 4) + (y0 + 1 + flip) % 2,
        )
        keys = jnp.concatenate([rop[at(p * 128, 128, 128), :] for p in pairs], axis=0)
        c = lax.dot_general(lop[...], keys, NT, preferred_element_type=F32).astype(BF)
        for q in range(2):
            for b in range(11):
                lhs2[q * 64 : q * 64 + 64, b * 128 : b * 128 + 128] = c[b * 64 : b * 64 + 64, q * 128 : q * 128 + 128]
        zs = []
        for t in range(4):
            lo, hi = SPAN[t]
            z = jnp.dot(lhs2[:, lo * 128 : hi * 128], s2[t, : (hi - lo) * 128, :], preferred_element_type=F32)
            zs.append(z.reshape(16, 8, 256))
        for h in range(2):
            z = jnp.concatenate([zs[2 * h], zs[2 * h + 1]], axis=1).astype(BF)
            for q in range(2):
                sb[h, at(pairs[q] * 8, 8, 8)] = z[8 * q : 8 * q + 8]

        for dr in range(ROWS):
            r = lax.rem(row + dr, ROWS)
            for k in range(2):
                for p in pairs:

                    def start(r=r, k=k, p=p):
                        pltpu.make_async_remote_copy(
                            src_ref=sb.at[:, p * 8 + r, :, k * 128 : k * 128 + 128], dst_ref=rv.at[me],
                            send_sem=c_send, recv_sem=c_recv.at[step], device_id=(r, 2 * p + k), device_id_type=MESH,
                        ).start()

                    if dr:
                        start()
                    else:
                        pl.when(2 * p + k != col)(start)
        return 0

    lax.fori_loop(0, 4, product, 0, unroll=2)
    back = sb.at[:, col // 2 * 8 + row, :, at(col % 2 * 128, 128, 128)]
    pltpu.make_async_copy(back, rv.at[me], c_recv.at[2]).start()

    for step in range(4):
        odd, flip = step % 2, step // 2
        part = rv.at[0 : N // 4]
        pltpu.make_async_copy(part, part, c_recv.at[step]).wait()
        for dx, dy in ((2 - odd, flip), (3 * odd, 1 + flip)):
            p = 2 * lax.rem(x + 4 - dx, 4) + lax.rem(y0 + dy, 2)

            def unpack(r, _, p=p):
                for k in range(2):
                    c = r * COLS + 2 * p + k
                    for h in range(2):
                        rc[h, at(c * PITCH2, 16, 8), :] = rv[c, h].astype(F32)
                return 0

            lax.fori_loop(0, ROWS, unpack, 0, unroll=4)

    def finish(ia, _):
        for t in range(4):
            z = rc[t // 2, pl.ds(t % 2 * 8 + ia, 128, stride=PITCH2), :]
            c = z - jnp.mean(z, axis=0, keepdims=True)
            n = (c * lax.rsqrt(jnp.mean(c * c, axis=0, keepdims=True) + 1e-05)).astype(BF)
            branch = lax.dot_general(n, wout[...], TN, preferred_element_type=F32)
            br[t * 128 : t * 128 + 128] = branch * gate[ia, t * 128 : t * 128 + 128]
        for ib in range(11):
            cells = pl.ds(44 * lax.div(ia, 4) + in_half(lax.rem(ia, 4), ib), CJ, stride=RI)
            psf[cells, :] = psf[cells, :] + br[44 * ib : 44 * ib + 44]
        return 0

    lax.fori_loop(0, 8, finish, 0, unroll=8)
    out[...] = psf[...].astype(BF).reshape(CJ, RI, 128)

    def sent(src, sem):
        pltpu.make_async_remote_copy(
            src_ref=src, dst_ref=src, send_sem=sem, recv_sem=l_recv, device_id=dev((me + 1) % N), device_id_type=MESH
        ).wait_send()

    sent(lmsg.at[0:7, 0], l_send)
    sent(rt.at[0:7], r1_send)
    sent(rmsg.at[0:240], r2_send)
    for m, (_, _, t_lo, t_hi) in enumerate(PARTS):
        sent(send.at[0 : N - 1, t_lo:t_hi], e_send.at[m])
    sent(rv.at[0 : N - 1], c_send)


def per_device(hf, ps, f1, f2, wo, wl, wr, wg, wout):
    dma = pltpu.SemaphoreType.DMA
    vm = pltpu.VMEM
    out = pl.pallas_call(
        kernel,
        out_shape=jax.ShapeDtypeStruct((CJ, RI, 128), BF),
        in_specs=[pl.BlockSpec(memory_space=pl.ANY)] * 9,
        out_specs=VM,
        scratch_shapes=[
            vm(hf.shape, BF), vm((CJ, RI, 128), BF), vm((32, 256), BF), vm((32, 256), BF), vm(wo.shape, BF),
            vm(wl.shape, BF), vm(wr.shape, BF), vm(wg.shape, BF), vm(wout.shape, BF),
            vm((96, 1024), F32), vm((128, 128), F32), vm((16, 768), BF), vm((2, 16, 384), F32), vm((2, 16, 384), BF),
            vm((8, 2, 16, 768), BF), vm((8, 2, 16, 384), BF), vm((256, 384), BF), vm((384, 256), BF), vm((1024, 128), F32),
            vm((4096, 512), BF), vm((576, 4096), BF), vm((576, 512), F32), vm((4, 1536, 256), BF), vm((CJ * RI, 128), F32),
            vm((8, 512, 128), F32), vm((2, 8 * PITCH, 128), F32), vm((2, 8 * PITCH, 128), F32), vm((512, 128), BF),
            vm((8, 512, 128), F32), vm((N, 4, 16, 128), BF), vm((4, 1024, 256), BF), vm((4, 256, 512), BF),
            vm((4, 512, 256), BF), vm((704, 1024), BF), vm((8, 1024, 128), F32), vm((1024, 1024), BF),
            vm((128, 1408), BF), vm((2, 64, 16, 256), BF), vm((N, 2, 16, 128), BF), vm((2, N * PITCH2, 128), F32),
            vm((512, 128), F32), dma((9,)), dma, dma, dma, dma, dma, dma, dma, dma, dma((2,)), dma((2,)), dma, dma((4,)),
        ],
        compiler_params=pltpu.CompilerParams(
            vmem_limit_bytes=60 * 2**20, collective_id=0, has_side_effects=True
        ),
    )(hf, ps.transpose(1, 0, 2), f1.T, f2.T, wo, wl, wr, wg, wout)
    return out.transpose(1, 0, 2)


def solution(mesh):
    return jax.shard_map(
        per_device,
        mesh=mesh,
        in_specs=(P("col", "row", None), P("row", "col", None), P(), P(), P(), P(), P(), P(), P()),
        out_specs=P("row", "col", None),
        check_vma=False,
    )
```
